32 devices in a mesh: groups: 2 (over y), seq: 4 (over z), tp: 2 (over x), section: 2 (over core).
Axes of the slice: x: 2, y: 2, z: 4, core: 2. Of those that a mesh axis runs over, the one named last changes fastest.
Arguments:
- page_pool: bfloat16 [384, 128, 576], P(('groups', 'seq', 'tp', 'section')), parts along dimension 0, as said below
- queries: bfloat16 [32, 64, 576], P(('groups', 'seq')), parts along dimension 0, as said below
- block_table: int32 [32, 2, 4], P(('groups', 'seq'), 'tp'), parts along dimension 0, may hold values from 0 to 11, as said below
- res_len: int32 [32, 2], P(('groups', 'seq'), 'tp'), parts along dimension 0, may hold values from 0 to 512, as said below
- piece_len: int32 [8, 2, 4], P(('groups', 'seq'), 'tp'), parts along dimension 0, may hold values from 1 to 512, 1024 in all within a row
- piece_owner: int32 [8, 2, 4], P(('groups', 'seq'), 'tp'), parts along dimension 0, may hold values from 0 to 3, each once within a row
- piece_slot: int32 [8, 2, 4], P(('groups', 'seq'), 'tp'), parts along dimension 0, may hold values from 0 to 3
- piece_pos: int32 [8, 2, 4], P(('groups', 'seq'), 'tp'), parts along dimension 0, may hold values from 0 to 8191
- kv_gain: float32 [512], replicated, may hold values from 0.25 to 1.75
Outputs:
- attended: bfloat16 [2, 32, 64, 512], P('section', ('groups', 'seq'), 'tp'), parts along dimension 1
The draws below stay inside these ranges and needn't reach their ends.
There are 2 independent parts, one for each index of `groups`. The reference program is written for one: setup_inputs(seed, part) draws one part's arguments, and reference() takes and returns one part's arrays. A program takes and returns all parts, laid end to end along the dimension named above; an argument that names none is the same for every part. Nothing has to cross between parts.
Inputs may be any that keep to these rules, and one draw needn't show every extreme that they name: `block_table`: on each tp index of a row, the first ceil(res_len / 128) entries name distinct pages of that decode device, distinct from those of its other rows; the rest name pages too. `res_len`: every row has resident tokens on some tp index; on every decode device one row holds exactly 512 tokens. `piece_len`: the pieces of one prefill device sum to 1024 tokens; on every device one piece has exactly 512. `piece_owner`: each prefill device has exactly one piece for every decode owner. `page_pool`: entries lie within -20 and 20. `queries`: entries lie within -12 and 12.
All inputs are finite; a program needn't handle non-finite values.
Results may differ from the reference program's by a relative error of at most 0.0027.
Values may be sent and summed in bfloat16 or wider, within the bound.
A program may use at most 64 MiB of HBM per device.

```python
import math
import jax
import jax.numpy as jnp
import numpy as np
from jax import lax

LAT = 512
HEADS = 64
PAGE = 128
MAXP_PAGES = 4
B_DEV = 4
FRESH_DEV = 1024
KVW = 576
MOSTLEN = 512
PAGES_DEV = 12
ROWS = 16
N_SEQ = 4
N_TP = 2
N_SECTION = 2


def resident_layout(key):
    key = jax.random.fold_in(key, 500)
    key_count, key_heavy, key_fill, key_order = jax.random.split(key, 4)
    row_ids = jnp.arange(ROWS, dtype=jnp.int32)
    tp_ids = jnp.arange(N_TP, dtype=jnp.int32)
    page_count = jax.random.randint(key_count, (ROWS, N_TP), 0, 2)
    forced = (row_ids[:, None] % N_TP == tp_ids[None, :]).astype(jnp.int32)
    page_count = jnp.maximum(page_count, forced)
    heavy_row = jax.random.randint(key_heavy, (N_SEQ, 1, N_TP), 0, B_DEV)
    row_within = (row_ids % B_DEV).reshape(N_SEQ, B_DEV, 1)
    is_heavy = (row_within == heavy_row).reshape(ROWS, N_TP)
    page_count = jnp.where(is_heavy, MAXP_PAGES, page_count)
    last_fill = jax.random.randint(key_fill, (ROWS, N_TP), 1, PAGE + 1)
    lengths = jnp.where(page_count > 0, (page_count - 1) * PAGE + last_fill, 0)
    lengths = jnp.where(is_heavy, MAXP_PAGES * PAGE, lengths)
    per_device = page_count.reshape(N_SEQ, B_DEV, N_TP)
    first_page = jnp.cumsum(per_device, axis=1) - per_device
    order_keys = jax.random.split(key_order, N_SEQ * N_TP)

    def one_order(order_key):
        return jax.random.permutation(order_key, PAGES_DEV)
    page_orders = jax.vmap(one_order)(order_keys).reshape(N_SEQ, 1, N_TP, PAGES_DEV)
    page_index = (first_page[:, :, :, None] + jnp.arange(MAXP_PAGES, dtype=jnp.int32)[None, None, None, :]) % PAGES_DEV
    widened = jnp.broadcast_to(page_orders, (N_SEQ, B_DEV, N_TP, PAGES_DEV))
    page_table = jnp.take_along_axis(widened, page_index, axis=3)
    return (page_table.reshape(ROWS, N_TP, MAXP_PAGES).astype(jnp.int32), lengths.astype(jnp.int32))


def draw_block_table(key, part):
    page_table, lengths = resident_layout(key)
    return page_table


def draw_res_len(key, part):
    page_table, lengths = resident_layout(key)
    return lengths


def draw_page_pool(key, part):
    key = jax.random.fold_in(key, 11)
    key_noise, key_scale = jax.random.split(key)
    noise_part = jax.random.truncated_normal(key_noise, -6.0, 6.0, (N_SEQ * N_TP * N_SECTION * PAGES_DEV, PAGE, KVW), jnp.float32)
    row_scale = jnp.exp(jax.random.uniform(key_scale, (N_SEQ * N_TP * N_SECTION * PAGES_DEV, PAGE, 1), jnp.float32, math.log(1.0 / 3.0), math.log(10.0 / 3.0)))
    values = row_scale * noise_part
    return values.astype(jnp.bfloat16)


def draw_queries(key, part):
    key = jax.random.fold_in(key, 12)
    key_noise = jax.random.fold_in(key, 0)
    noise_part = jax.random.truncated_normal(key_noise, -6.0, 6.0, (ROWS, HEADS, KVW), jnp.float32)
    values = noise_part
    return values.astype(jnp.bfloat16)


def place_ends(array, own_key, low, high):
    longest = array.shape.index(max(array.shape))
    spots = []
    for shift in (0, 1):
        where = [jax.random.randint(jax.random.fold_in(own_key, axis), (), 0, length) for axis, length in enumerate(array.shape)]
        where[longest] = (where[longest] + shift) % array.shape[longest]
        spots.append(tuple(where))
    return array.at[spots[0]].set(low).at[spots[1]].set(high)


def profile(amount, total, most, skew):
    weights = [(1 << 20) // math.isqrt(rank ** skew) + 1 for rank in range(2, amount + 1)]
    surplus, counts = total - most - (amount - 1), [1] * (amount - 1)
    while surplus > 0:
        free = [i for i in range(amount - 1) if counts[i] < most]
        pool, left = sum([weights[i] for i in free]), surplus
        for i in free:
            more = min(most - counts[i], max(1, left * weights[i] // pool), surplus)
            counts[i] = counts[i] + more
            surplus = surplus - more
    return np.array([most] + counts)


def uneven(stream_key, number_of, total, limit, lean):
    if number_of == 2:
        one = jax.random.randint(stream_key, (), max(1, total - limit), min(limit, total - 1) + 1)
        return jnp.stack([one, total - one])
    tallies = jnp.asarray(profile(number_of, total, limit, lean), jnp.int32)
    couples = (number_of - 1) // 2
    donor, taker = tallies[1:1 + 2 * couples:2], tallies[2:2 + 2 * couples:2]
    margin = jnp.minimum(donor - 1, limit - taker)
    moved = jax.random.randint(jax.random.fold_in(stream_key, 1), (couples,), 0, 1 << 20) % (margin + 1)
    tallies = tallies.at[1:1 + 2 * couples:2].set(donor - moved).at[2:2 + 2 * couples:2].set(taker + moved)
    return tallies[jax.random.permutation(jax.random.fold_in(stream_key, 2), number_of)]


def setup_inputs(seed: int = 0, part: int = 0) -> dict:
    splits = jax.random.split(jax.random.key(seed), 10)
    part_keys = jax.random.split(jax.random.fold_in(splits[9], part), 10)
    page_pool = draw_page_pool(jax.random.fold_in(jax.random.fold_in(splits[9], part), 71), part)
    queries = draw_queries(jax.random.fold_in(jax.random.fold_in(splits[9], part), 71), part)
    block_table = draw_block_table(jax.random.fold_in(jax.random.fold_in(splits[9], part), 71), part)
    res_len = draw_res_len(jax.random.fold_in(jax.random.fold_in(splits[9], part), 71), part)
    piece_len = jax.vmap(lambda own: uneven(own, N_SEQ, FRESH_DEV, MOSTLEN, 2))(jax.random.split(part_keys[4], N_SEQ * N_TP)).reshape((N_SEQ, N_TP, N_SEQ)).astype(jnp.int32)
    piece_owner = jax.vmap(lambda own: jax.random.permutation(own, N_SEQ))(jax.random.split(part_keys[5], N_SEQ * N_TP)).reshape((N_SEQ, N_TP, N_SEQ)).astype(jnp.int32)
    piece_slot = place_ends(jax.random.randint(part_keys[6], (N_SEQ, N_TP, N_SEQ), 0, B_DEV), jax.random.fold_in(part_keys[6], 1), 0, B_DEV - 1).astype(jnp.int32)
    piece_pos = place_ends(jax.random.randint(part_keys[7], (N_SEQ, N_TP, N_SEQ), 0, 8192), jax.random.fold_in(part_keys[7], 1), 0, 8191).astype(jnp.int32)
    kv_gain = jnp.clip(1.0 + 0.15 * jax.random.normal(splits[8], (LAT,), jnp.float32), 0.25, 1.75)
    return {"page_pool": page_pool, "queries": queries, "block_table": block_table, "res_len": res_len, "piece_len": piece_len, "piece_owner": piece_owner, "piece_slot": piece_slot, "piece_pos": piece_pos, "kv_gain": kv_gain}


SOFT_SCALE = 192.0 ** (-0.5)
MASKED = -1e+30
NORM_EPSILON = 1e-06

def rotate_half(rope_part, positions):
    half_width = rope_part.shape[-1] // 2
    inverse = 10000.0 ** (-jnp.arange(half_width, dtype=jnp.float32) / half_width)
    angles = positions.astype(jnp.float32)[:, None] * inverse[None, :]
    cosine = jnp.cos(angles)
    sine_part = jnp.sin(angles)
    first_half = rope_part[:, :half_width]
    second_half = rope_part[:, half_width:]
    return jnp.concatenate([first_half * cosine - second_half * sine_part, second_half * cosine + first_half * sine_part], axis=1)

def prepare_fresh(raw_tokens, kv_gain, piece_len, piece_pos):
    latent_width = kv_gain.shape[0]
    token_ids = jnp.arange(raw_tokens.shape[0], dtype=jnp.int32)
    piece_end = jnp.cumsum(piece_len).astype(jnp.int32)
    piece_begin = piece_end - piece_len
    owning = lax.optimization_barrier(jnp.sum((token_ids[:, None] >= piece_end[None, :]).astype(jnp.int32), axis=1))
    selector = (owning[:, None] == jnp.arange(piece_len.shape[0], dtype=jnp.int32)[None, :]).astype(jnp.int32)
    positions = lax.optimization_barrier(jnp.sum(selector * (piece_pos - piece_begin)[None, :], axis=1)) + token_ids
    values = raw_tokens.astype(jnp.float32)
    latent = values[:, :latent_width]
    square_mean = lax.optimization_barrier(jnp.mean(latent * latent, axis=1, keepdims=True))
    normed = latent * lax.rsqrt(square_mean + NORM_EPSILON) * kv_gain[None, :]
    rotated = rotate_half(values[:, latent_width:], positions)
    return jnp.concatenate([normed, rotated], axis=1).astype(jnp.bfloat16)

def part_softmax(query_rows, key_rows, live_count, latent_width):
    wide_query = query_rows.astype(jnp.float32)
    wide_keys = key_rows.astype(jnp.float32)
    scores = jnp.einsum('bhc,bkc->bhk', wide_query, wide_keys, precision=lax.Precision.HIGHEST) * SOFT_SCALE
    is_live = (jnp.arange(key_rows.shape[1], dtype=jnp.int32)[None, :] < live_count[:, None])[:, None, :]
    scores = jnp.where(is_live, scores, MASKED)
    row_max = lax.optimization_barrier(jnp.max(scores, axis=2))
    weights = jnp.where(is_live, jnp.exp(scores - row_max[:, :, None]), 0.0)
    row_total = lax.optimization_barrier(jnp.sum(weights, axis=2))
    rounded = lax.optimization_barrier(weights.astype(jnp.bfloat16)).astype(jnp.float32)
    row_out = jnp.einsum('bhk,bkv->bhv', rounded, wide_keys[:, :, :latent_width], precision=lax.Precision.HIGHEST)
    return (row_max, row_total, row_out)

def owner_parts(query_rows, page_block, page_table, res_lens, handed, slot_ids, handed_len, latent_width):
    row_count = query_rows.shape[0]
    gathered = page_block[page_table].reshape(row_count, -1, page_block.shape[2])
    res_max, res_total, res_out = part_softmax(query_rows, gathered, res_lens, latent_width)
    piece_max, piece_total, piece_out = part_softmax(query_rows[slot_ids], handed, handed_len, latent_width)
    member = (slot_ids[None, :] == jnp.arange(row_count, dtype=jnp.int32)[:, None])[:, :, None]
    row_max = jnp.maximum(res_max, lax.optimization_barrier(jnp.max(jnp.where(member, piece_max[None], MASKED), axis=1)))
    res_weight = jnp.exp(res_max - row_max)
    piece_weight = jnp.exp(jnp.where(member, piece_max[None] - row_max[:, None], MASKED))
    row_total = res_total * res_weight + jnp.einsum('rbh,bh->rh', piece_weight, piece_total, precision=lax.Precision.HIGHEST)
    row_out = res_out * res_weight[:, :, None] + jnp.einsum('rbh,bhv->rhv', piece_weight, piece_out, precision=lax.Precision.HIGHEST)
    return (row_max, row_total, row_out)

def reference(page_pool, queries, block_table, res_len, piece_len, piece_owner, piece_slot, piece_pos, kv_gain):
    latent_width = kv_gain.shape[0]
    pools = page_pool.reshape(N_SEQ, N_TP, N_SECTION, PAGES_DEV * PAGE, KVW)
    raw_all = pools[:, :, 0, :FRESH_DEV].reshape(N_SEQ * N_TP, FRESH_DEV, KVW)

    def prepare_one(operands):
        raw_tokens, lengths, positions = operands
        return prepare_fresh(raw_tokens, kv_gain, lengths, positions)
    fresh = lax.map(prepare_one, (raw_all, piece_len.reshape(N_SEQ * N_TP, N_SEQ), piece_pos.reshape(N_SEQ * N_TP, N_SEQ)))
    fresh = fresh.reshape(N_SEQ, N_TP, FRESH_DEV, KVW)
    piece_begin = (jnp.cumsum(piece_len, axis=2) - piece_len).astype(jnp.int32)
    columns = jnp.arange(MOSTLEN, dtype=jnp.int32)
    source_ids = jnp.arange(N_SEQ, dtype=jnp.int32)

    def owner_rows(owner):
        query_rows = lax.dynamic_slice_in_dim(queries, owner * B_DEV, B_DEV, 0)
        tables = lax.dynamic_slice_in_dim(block_table, owner * B_DEV, B_DEV, 0)
        resident = lax.dynamic_slice_in_dim(res_len, owner * B_DEV, B_DEV, 0)

        def tp_parts(tp_index):
            page_block = pools[owner, tp_index, 1].reshape(PAGES_DEV, PAGE, KVW)
            matches = (piece_owner[:, tp_index, :] == owner).astype(jnp.int32)
            handed_len = lax.optimization_barrier(jnp.sum(matches * piece_len[:, tp_index, :], axis=1))
            handed_begin = lax.optimization_barrier(jnp.sum(matches * piece_begin[:, tp_index, :], axis=1))
            handed_slot = lax.optimization_barrier(jnp.sum(matches * piece_slot[:, tp_index, :], axis=1))
            token_index = jnp.minimum(handed_begin[:, None] + columns[None, :], FRESH_DEV - 1)
            handed = fresh[source_ids[:, None], tp_index, token_index]
            return owner_parts(query_rows, page_block, tables[:, tp_index], resident[:, tp_index], handed, handed_slot, handed_len, latent_width)
        part_max, part_total, part_out = lax.map(tp_parts, jnp.arange(N_TP, dtype=jnp.int32))
        row_max = lax.optimization_barrier(jnp.max(part_max, axis=0))
        part_weight = jnp.exp(part_max - row_max[None])
        row_total = lax.optimization_barrier(jnp.sum(part_total * part_weight, axis=0))
        row_out = lax.optimization_barrier(jnp.sum(part_out * part_weight[:, :, :, None], axis=0))
        return (row_out / row_total[:, :, None]).astype(jnp.bfloat16)
    attended = lax.map(owner_rows, jnp.arange(N_SEQ, dtype=jnp.int32)).reshape(ROWS, HEADS, LAT)
    return jnp.stack([jnp.zeros_like(attended), attended], axis=0)
```

```python
import functools

import jax
import jax.numpy as jnp
import numpy as np
from jax import lax
from jax.experimental import pallas as pl
from jax.experimental.pallas import tpu as pltpu
from jax.sharding import PartitionSpec as P

FRESH_DEV = 1024
SOFT_SCALE = 192.0 ** (-0.5)
MASKED = -1e30
NORM_EPSILON = 1e-06
GROUP = 4
MESH = pl.DeviceIdType.MESH


def stats_block(out, row_max, row_total, slot):
    lane = lax.broadcasted_iota(jnp.int32, (out.shape[0], 128), 1)
    return jnp.where(lane == 0, row_max, jnp.where(lane == 1, row_total, slot))


def kernel(
    n_seq, n_tp, pool_ref, q_ref, table_ref, res_ref, len_ref, owner_ref, slot_ref, pos_ref,
    gain_ref, freq_ref, out_ref,
    pool, fresh, q_in, q_out, meta_in, meta_out, weights, piece_out, piece_in, res_out, res_in,
    pool_sem, meta_send, meta_recv, q_send, q_recv, piece_send, piece_recv, res_send, res_recv,
):
    pages, width, page = pool.shape
    rows, heads, _ = q_ref.shape
    latent = gain_ref.shape[1]
    half = (width - latent) // 2
    share = heads // n_tp
    fresh_pages = FRESH_DEV // page
    seq = lax.axis_index("seq")
    tp = lax.axis_index("tp")
    section = lax.axis_index("section")
    barrier = pltpu.get_barrier_semaphore()

    def at(s, t, c):
        return {"seq": s, "tp": t, "section": c}

    def meta_copy(peer, own):
        return pltpu.make_async_remote_copy(
            meta_out.at[peer], meta_in.at[own], meta_send.at[peer], meta_recv.at[own],
            device_id=at(peer, tp, 0), device_id_type=MESH,
        )

    def q_copy(peer, own):
        return pltpu.make_async_remote_copy(
            q_out.at[peer], q_in.at[own], q_send.at[peer], q_recv.at[own],
            device_id=at(peer, tp, 0), device_id_type=MESH,
        )

    def piece_copy(d, t, own):
        return pltpu.make_async_remote_copy(
            piece_out.at[d, t], piece_in.at[own], piece_send.at[d * n_tp + t], piece_recv.at[own],
            device_id=at(d, t, 1), device_id_type=MESH,
        )

    def res_copy(t, own):
        return pltpu.make_async_remote_copy(
            res_out.at[t], res_in.at[own], res_send.at[t], res_recv.at[own],
            device_id=at(seq, t, 1), device_id_type=MESH,
        )

    @pl.when(section == 0)
    def prefill():
        raw_copy = pltpu.make_async_copy(
            pool_ref.at[pl.ds(0, fresh_pages)], pool.at[pl.ds(0, fresh_pages)], pool_sem
        )
        raw_copy.start()
        for k in range(1, n_seq):
            pl.semaphore_signal(
                barrier, inc=1, device_id=at(lax.rem(seq + k, n_seq), tp, 0), device_id_type=MESH
            )

        lengths = [len_ref[0, 0, k] for k in range(n_seq)]
        begins = [jnp.int32(0)]
        for k in range(n_seq - 1):
            begins.append(begins[-1] + lengths[k])

        def of_owner(d, values):
            total = jnp.int32(0)
            for k in range(n_seq):
                total = total + jnp.where(owner_ref[0, 0, k] == d, values[k], 0)
            return total

        slots = [slot_ref[0, 0, k] for k in range(n_seq)]
        owner_begin = [of_owner(d, begins) for d in range(n_seq)]
        owner_len = [of_owner(d, lengths) for d in range(n_seq)]
        owner_slot = [of_owner(d, slots) for d in range(n_seq)]
        for d in range(n_seq):
            meta_out[d] = jnp.full(meta_out.shape[1:], owner_slot[d], jnp.int32)

        pl.semaphore_wait(barrier, n_seq - 1 + n_seq * n_tp)
        for k in range(1, n_seq):
            meta_copy(lax.rem(seq + k, n_seq), seq).start()

        turns = []
        for j in range(fresh_pages):
            token = lax.broadcasted_iota(jnp.int32, (1, page), 1) + j * page
            shift = jnp.zeros((1, page), jnp.int32)
            for k in range(n_seq):
                live = (token >= begins[k]) & (token < begins[k] + lengths[k])
                shift = jnp.where(live, pos_ref[0, 0, k] - begins[k], shift)
            angles = (token + shift).astype(jnp.float32) * freq_ref[...]
            turns.append((jnp.cos(angles), jnp.sin(angles)))

        for k in range(1, n_seq):
            peer = lax.rem(seq + k, n_seq)
            meta_copy(peer, peer).wait_recv()
            wanted = meta_in[peer][0:1, 0:1]
            picked = q_ref[0].astype(jnp.float32)
            for r in range(1, rows):
                picked = jnp.where(wanted == r, q_ref[r].astype(jnp.float32), picked)
            q_out[peer] = picked.astype(jnp.bfloat16)
            q_copy(peer, seq).start()
        own_slot = meta_out[seq][0:1, 0:1]
        picked = q_ref[0].astype(jnp.float32)
        for r in range(1, rows):
            picked = jnp.where(own_slot == r, q_ref[r].astype(jnp.float32), picked)
        q_in[seq] = picked.astype(jnp.bfloat16)

        raw_copy.wait()
        gain = jnp.broadcast_to(gain_ref[...], (page, latent)).T
        for j in range(fresh_pages):
            x = pool[j, :latent].astype(jnp.float32)
            mean = jnp.mean(x * x, axis=0, keepdims=True)
            columns = slice(j * page, (j + 1) * page)
            normed = x * lax.rsqrt(mean + NORM_EPSILON) * gain
            fresh[:latent, columns] = normed.astype(jnp.bfloat16)
            y = pool[j, latent:].astype(jnp.float32)
            a, b = y[:half], y[half:]
            cosine, sine = turns[j]
            turned = jnp.concatenate([a * cosine - b * sine, b * cosine + a * sine], axis=0)
            fresh[latent:, columns] = turned.astype(jnp.bfloat16)

        out_ref[...] = jnp.zeros_like(out_ref)
        for k in range(1, n_seq):
            peer = lax.rem(seq + k, n_seq)
            q_copy(peer, peer).wait_recv()

        tokens = lax.broadcasted_iota(jnp.int32, (1, FRESH_DEV), 1)
        for first in range(0, n_seq, GROUP):
            scores = (
                jnp.dot(
                    q_in[first : first + GROUP].reshape(GROUP * heads, width),
                    fresh[...],
                    preferred_element_type=jnp.float32,
                )
                * SOFT_SCALE
            )
            stats = []
            for i in range(GROUP):
                d = first + i
                live = (tokens >= owner_begin[d]) & (tokens < owner_begin[d] + owner_len[d])
                part = jnp.where(live, scores[i * heads : (i + 1) * heads], MASKED)
                row_max = jnp.max(part, axis=1, keepdims=True)
                e = jnp.where(live, jnp.exp(part - row_max), 0.0)
                row_total = jnp.sum(e, axis=1, keepdims=True)
                weights[i * heads : (i + 1) * heads] = e.astype(jnp.bfloat16)
                stats.append(
                    stats_block(e, row_max, row_total, owner_slot[d].astype(jnp.float32))
                )
            for i in range(GROUP):
                d = first + i
                part_out = lax.dot_general(
                    weights[i * heads : (i + 1) * heads], fresh[:latent],
                    (((1,), (1,)), ((), ())), preferred_element_type=jnp.float32,
                )
                for t in range(n_tp):
                    mine = slice(t * share, (t + 1) * share)
                    piece_out[d, t, :, :latent] = part_out[mine]
                    piece_out[d, t, :, latent:] = stats[i][mine]
                    piece_copy(d, t, seq * n_tp + tp).start()

        for k in range(1, n_seq):
            peer = lax.rem(seq + k, n_seq)
            meta_copy(peer, peer).wait_send()
            q_copy(peer, peer).wait_send()
        for d in range(n_seq):
            for t in range(n_tp):
                piece_copy(d, t, 0).wait_send()

    @pl.when(section == 1)
    def decode():
        pool_copy = pltpu.make_async_copy(pool_ref, pool, pool_sem)
        pool_copy.start()
        for s in range(n_seq):
            for t in range(n_tp):
                pl.semaphore_signal(barrier, inc=1, device_id=at(s, t, 0), device_id_type=MESH)
        for k in range(1, n_tp):
            pl.semaphore_signal(
                barrier, inc=1, device_id=at(seq, lax.rem(tp + k, n_tp), 1), device_id_type=MESH
            )
        pool_copy.wait()
        most = table_ref.shape[2]
        tokens = lax.broadcasted_iota(jnp.int32, (1, most * page), 1)
        for r in range(rows):
            keys = jnp.concatenate([pool[table_ref[r, 0, j]] for j in range(most)], axis=1)
            scores = jnp.dot(q_ref[r], keys, preferred_element_type=jnp.float32) * SOFT_SCALE
            live = tokens < res_ref[r, 0]
            scores = jnp.where(live, scores, MASKED)
            row_max = jnp.max(scores, axis=1, keepdims=True)
            e = jnp.where(live, jnp.exp(scores - row_max), 0.0)
            row_total = jnp.sum(e, axis=1, keepdims=True)
            part_out = lax.dot_general(
                e.astype(jnp.bfloat16), keys[:latent],
                (((1,), (1,)), ((), ())), preferred_element_type=jnp.float32,
            )
            stats = stats_block(e, row_max, row_total, 0.0)
            for t in range(n_tp):
                mine = slice(t * share, (t + 1) * share)
                res_out[t, r, :, :latent] = part_out[mine]
                res_out[t, r, :, latent:] = stats[mine]
        if n_tp > 1:
            pl.semaphore_wait(barrier, n_tp - 1)
        for k in range(1, n_tp):
            res_copy(lax.rem(tp + k, n_tp), tp).start()
        res_in[tp] = res_out[tp]
        for k in range(1, n_tp):
            peer = lax.rem(tp + k, n_tp)
            res_copy(peer, peer).wait_recv()
        for p in range(n_seq * n_tp):
            piece_copy(0, 0, p).wait_recv()

        piece_max = [piece_in[p, :, latent : latent + 1] for p in range(n_seq * n_tp)]
        piece_total = [piece_in[p, :, latent + 1 : latent + 2] for p in range(n_seq * n_tp)]
        piece_slot = [piece_in[p, :, latent + 2 : latent + 3] for p in range(n_seq * n_tp)]
        for r in range(rows):
            parts = [res_in[t, r, :, latent : latent + 1] for t in range(n_tp)]
            parts += [
                jnp.where(piece_slot[p] == float(r), piece_max[p], MASKED)
                for p in range(n_seq * n_tp)
            ]
            joint = functools.reduce(jnp.maximum, parts)
            total = jnp.zeros((share, 1), jnp.float32)
            out = jnp.zeros((share, latent), jnp.float32)
            for t in range(n_tp):
                scale = jnp.exp(parts[t] - joint)
                total += res_in[t, r, :, latent + 1 : latent + 2] * scale
                out += res_in[t, r, :, :latent] * scale
            for p in range(n_seq * n_tp):
                scale = jnp.where(
                    piece_slot[p] == float(r), jnp.exp(parts[n_tp + p] - joint), 0.0
                )
                total += piece_total[p] * scale
                out += piece_in[p, :, :latent] * scale
            out_ref[0, r] = (out / total).astype(jnp.bfloat16)
        for k in range(1, n_tp):
            res_copy(lax.rem(tp + k, n_tp), tp).wait_send()


def local(
    n_seq, n_tp,
    page_pool, queries, block_table, res_len, piece_len, piece_owner, piece_slot, piece_pos, kv_gain
):
    pages, page, width = page_pool.shape
    rows, heads, _ = queries.shape
    latent = kv_gain.shape[0]
    half = (width - latent) // 2
    share = heads // n_tp
    freq = np.float64(10000.0) ** (-np.arange(half) / half)
    freq = jnp.asarray(np.broadcast_to(freq.astype(np.float32)[:, None], (half, page)))
    vmem = pl.BlockSpec(memory_space=pltpu.VMEM)
    smem = pl.BlockSpec(memory_space=pltpu.SMEM)
    parts = n_seq * n_tp
    return pl.pallas_call(
        functools.partial(kernel, n_seq, n_tp),
        out_shape=jax.ShapeDtypeStruct((1, rows, share, latent), jnp.bfloat16),
        in_specs=[pl.BlockSpec(memory_space=pl.ANY), vmem] + [smem] * 6 + [vmem, vmem],
        out_specs=vmem,
        scratch_shapes=[
            pltpu.VMEM((pages, width, page), jnp.bfloat16),
            pltpu.VMEM((width, FRESH_DEV), jnp.bfloat16),
            pltpu.VMEM((n_seq, heads, width), jnp.bfloat16),
            pltpu.VMEM((n_seq, heads, width), jnp.bfloat16),
            pltpu.VMEM((n_seq, 8, 128), jnp.int32),
            pltpu.VMEM((n_seq, 8, 128), jnp.int32),
            pltpu.VMEM((GROUP * heads, FRESH_DEV), jnp.bfloat16),
            pltpu.VMEM((n_seq, n_tp, share, latent + 128), jnp.float32),
            pltpu.VMEM((parts, share, latent + 128), jnp.float32),
            pltpu.VMEM((n_tp, rows, share, latent + 128), jnp.float32),
            pltpu.VMEM((n_tp, rows, share, latent + 128), jnp.float32),
            pltpu.SemaphoreType.DMA,
            pltpu.SemaphoreType.DMA((n_seq,)),
            pltpu.SemaphoreType.DMA((n_seq,)),
            pltpu.SemaphoreType.DMA((n_seq,)),
            pltpu.SemaphoreType.DMA((n_seq,)),
            pltpu.SemaphoreType.DMA((parts,)),
            pltpu.SemaphoreType.DMA((parts,)),
            pltpu.SemaphoreType.DMA((n_tp,)),
            pltpu.SemaphoreType.DMA((n_tp,)),
        ],
        compiler_params=pltpu.CompilerParams(
            collective_id=0, has_side_effects=True, vmem_limit_bytes=48 * 1024 * 1024
        ),
    )(
        jnp.swapaxes(page_pool, 1, 2), queries, block_table, res_len, piece_len, piece_owner,
        piece_slot, piece_pos, kv_gain[None], freq,
    )


def solution(mesh):
    return jax.shard_map(
        functools.partial(local, mesh.shape["seq"], mesh.shape["tp"]),
        mesh=mesh,
        in_specs=(
            P(("groups", "seq", "tp", "section"), None, None),
            P(("groups", "seq"), None, None),
            P(("groups", "seq"), "tp", None),
            P(("groups", "seq"), "tp"),
            P(("groups", "seq"), "tp", None),
            P(("groups", "seq"), "tp", None),
            P(("groups", "seq"), "tp", None),
            P(("groups", "seq"), "tp", None),
            P(),
        ),
        out_specs=P("section", ("groups", "seq"), "tp", None),
        check_vma=False,
    )
```

```python
import functools

import jax
import jax.numpy as jnp
import numpy as np
from jax import lax
from jax.experimental import pallas as pl
from jax.experimental.pallas import tpu as pltpu
from jax.sharding import PartitionSpec as P

FRESH_DEV = 1024
SOFT_SCALE = 192.0 ** (-0.5)
MASKED = -1e30
NORM_EPSILON = 1e-06
GROUP = 2
MESH = pl.DeviceIdType.MESH


def stats_rows(row_max, row_total, slot):
    lane = lax.broadcasted_iota(jnp.int32, (row_max.shape[0], 128), 1)
    block = jnp.where(lane == 0, row_max, jnp.where(lane == 1, row_total, slot))
    return block.T[:8]


def cos_sin(angles):
    turns = jnp.floor(angles * (2.0 / np.pi) + 0.5)
    rest = angles - turns * 1.5703125
    rest = rest - turns * 4.837512969970703125e-4
    rest = rest - turns * 7.54978995489188216e-8
    square = rest * rest
    sine = rest + rest * square * (
        -1.6666654611e-1 + square * (8.3321608736e-3 + square * -1.9515295891e-4)
    )
    cosine = (
        1.0
        - 0.5 * square
        + square * square
        * (4.166664568298827e-2 + square * (-1.388731625493765e-3 + square * 2.443315711809948e-5))
    )
    quarter = turns.astype(jnp.int32) & 3
    odd = (quarter & 1) == 1
    cos_value = jnp.where(odd, sine, cosine)
    sin_value = jnp.where(odd, cosine, sine)
    cos_value = jnp.where((quarter == 1) | (quarter == 2), -cos_value, cos_value)
    sin_value = jnp.where(quarter >= 2, -sin_value, sin_value)
    return cos_value, sin_value


def kernel(
    n_seq, n_tp, pool_hbm, q_hbm, table_hbm, res_hbm, len_hbm, owner_hbm, slot_hbm, pos_hbm,
    gain_hbm, out_ref,
    q_ref, table_ref, res_ref, len_ref, owner_ref, slot_ref, pos_ref, gain_ref, load_sem,
    pool, fresh, q_in, q_out, meta_in, meta_out, piece_out, piece_in, res_out, res_in, res_sum,
    pool_sem, meta_send, meta_recv, q_send, q_recv, piece_send, piece_recv, res_send, res_recv,
):
    pages, width, page = pool.shape
    rows, heads, _ = q_ref.shape
    latent = gain_ref.shape[1]
    half = (width - latent) // 2
    share = heads // n_tp
    fresh_pages = FRESH_DEV // page
    chunks = latent // 128
    seq = lax.axis_index("seq")
    tp = lax.axis_index("tp")
    section = lax.axis_index("section")
    barrier = pltpu.get_barrier_semaphore()
    order = [lax.rem((seq // 2) * 2 + 2 + i, n_seq) for i in range(n_seq)]
    peers = order[: n_seq - 2] + [(seq // 2) * 2 + 1 - lax.rem(seq, 2)]

    loads = [
        pltpu.make_async_copy(source, target, load_sem.at[i])
        for i, (source, target) in enumerate(
            [
                (len_hbm, len_ref), (owner_hbm, owner_ref), (slot_hbm, slot_ref),
                (pos_hbm, pos_ref), (table_hbm, table_ref), (res_hbm, res_ref),
                (q_hbm, q_ref), (gain_hbm, gain_ref),
            ]
        )
    ]
    for load in loads:
        load.start()

    def at(s, t, c):
        return {"seq": s, "tp": t, "section": c}

    def meta_copy(peer, own):
        return pltpu.make_async_remote_copy(
            meta_out.at[peer], meta_in.at[own], meta_send.at[peer], meta_recv.at[own],
            device_id=at(peer, tp, 0), device_id_type=MESH,
        )

    def q_copy(peer, own):
        return pltpu.make_async_remote_copy(
            q_out.at[peer], q_in.at[own], q_send.at[peer], q_recv.at[own],
            device_id=at(peer, tp, 0), device_id_type=MESH,
        )

    def piece_copy(i, t, own):
        return pltpu.make_async_remote_copy(
            piece_out.at[i, t], piece_in.at[own], piece_send.at[i * n_tp + t], piece_recv.at[own],
            device_id=at(order[i], t, 1), device_id_type=MESH,
        )

    def res_copy(t, own):
        return pltpu.make_async_remote_copy(
            res_out.at[t], res_in.at[own], res_send.at[t], res_recv.at[own],
            device_id=at(seq, t, 1), device_id_type=MESH,
        )

    @pl.when(section == 0)
    def prefill():
        raw_copy = pltpu.make_async_copy(
            pool_hbm.at[pl.ds(0, fresh_pages)], pool.at[pl.ds(0, fresh_pages)], pool_sem
        )
        raw_copy.start()
        for peer in peers:
            pl.semaphore_signal(barrier, inc=1, device_id=at(peer, tp, 0), device_id_type=MESH)
        for load in loads:
            load.wait()

        lengths = [len_ref[0, 0, k] for k in range(n_seq)]
        begins = [jnp.int32(0)]
        for k in range(n_seq - 1):
            begins.append(begins[-1] + lengths[k])

        def of_owner(d, values):
            total = jnp.int32(0)
            for k in range(n_seq):
                total = total + jnp.where(owner_ref[0, 0, k] == d, values[k], 0)
            return total

        slots = [slot_ref[0, 0, k] for k in range(n_seq)]
        owner_begin = [of_owner(d, begins) for d in order]
        owner_len = [of_owner(d, lengths) for d in order]
        owner_slot = [of_owner(d, slots) for d in order]
        for i, d in enumerate(order):
            meta_out[d] = jnp.full(meta_out.shape[1:], owner_slot[i], jnp.int32)

        pl.semaphore_wait(barrier, n_seq - 1 + n_seq * n_tp)
        for peer in peers:
            meta_copy(peer, seq).start()

        for peer in peers:
            meta_copy(peer, peer).wait_recv()
            wanted = meta_in[peer][0:1, 0:1]
            picked = q_ref[0].astype(jnp.float32)
            for r in range(1, rows):
                picked = jnp.where(wanted == r, q_ref[r].astype(jnp.float32), picked)
            q_out[peer] = picked.astype(jnp.bfloat16)
            q_copy(peer, seq).start()
        own_slot = meta_out[seq][0:1, 0:1]
        picked = q_ref[0].astype(jnp.float32)
        for r in range(1, rows):
            picked = jnp.where(own_slot == r, q_ref[r].astype(jnp.float32), picked)
        q_in[seq] = picked.astype(jnp.bfloat16)

        out_ref[...] = jnp.zeros_like(out_ref)
        raw_copy.wait()
        gain = jnp.broadcast_to(gain_ref[...], (page, latent)).T
        index = lax.broadcasted_iota(jnp.int32, (half, page), 0)
        freq = jnp.ones((half, page), jnp.float32)
        for i in range(1, half):
            freq = jnp.where(index == i, float(10000.0 ** (-i / half)), freq)
        for j in range(fresh_pages):
            x = pool[j, :latent].astype(jnp.float32)
            mean = jnp.mean(x * x, axis=0, keepdims=True)
            columns = slice(j * page, (j + 1) * page)
            normed = x * lax.rsqrt(mean + NORM_EPSILON) * gain
            fresh[:latent, columns] = normed.astype(jnp.bfloat16)
            y = pool[j, latent:].astype(jnp.float32)
            a, b = y[:half], y[half:]
            token = lax.broadcasted_iota(jnp.int32, (1, page), 1) + j * page
            shift = jnp.zeros((1, page), jnp.int32)
            for k in range(n_seq):
                live = (token >= begins[k]) & (token < begins[k] + lengths[k])
                shift = jnp.where(live, pos_ref[0, 0, k] - begins[k], shift)
            cosine, sine = cos_sin((token + shift).astype(jnp.float32) * freq)
            turned = jnp.concatenate([a * cosine - b * sine, b * cosine + a * sine], axis=0)
            fresh[latent:, columns] = turned.astype(jnp.bfloat16)

        out_ref[...] = jnp.zeros_like(out_ref)
        tokens = lax.broadcasted_iota(jnp.int32, (1, FRESH_DEV), 1)
        for first in range(0, n_seq, GROUP):
            for d in peers[first : first + GROUP]:
                q_copy(d, d).wait_recv()
            members = range(first, first + GROUP)
            wide = jnp.concatenate([q_in[order[i]] for i in members], axis=0)
            scores = jnp.dot(wide, fresh[...], preferred_element_type=jnp.float32) * SOFT_SCALE
            stats = []
            weights = []
            for i in members:
                live = (tokens >= owner_begin[i]) & (tokens < owner_begin[i] + owner_len[i])
                here = (i - first) * heads
                part = jnp.where(live, scores[here : here + heads], MASKED)
                row_max = jnp.max(part, axis=1, keepdims=True)
                e = jnp.where(live, jnp.exp(part - row_max), 0.0)
                row_total = jnp.sum(e, axis=1, keepdims=True)
                weights.append(e.astype(jnp.bfloat16))
                stats.append((row_max, row_total, owner_slot[i].astype(jnp.float32)))
            group_out = lax.dot_general(
                jnp.concatenate(weights, axis=0), fresh[:latent],
                (((1,), (1,)), ((), ())), preferred_element_type=jnp.float32,
            )
            for i in members:
                for t in range(n_tp):
                    here = (i - first) * heads + t * share
                    mine = slice(t * share, (t + 1) * share)
                    for c in range(chunks):
                        piece_out[i, t, c * share : (c + 1) * share] = group_out[
                            here : here + share, c * 128 : (c + 1) * 128
                        ]
                    row_max, row_total, slot = stats[i - first]
                    piece_out[i, t, chunks * share :, :share] = stats_rows(
                        row_max[mine], row_total[mine], slot
                    )
                    piece_copy(i, t, seq * n_tp + tp).start()

        for peer in peers:
            meta_copy(peer, peer).wait_send()
            q_copy(peer, peer).wait_send()
        for d in range(n_seq):
            for t in range(n_tp):
                piece_copy(d, t, 0).wait_send()

    @pl.when(section == 1)
    def decode():
        pool_copy = pltpu.make_async_copy(pool_hbm, pool, pool_sem)
        pool_copy.start()
        for s in range(n_seq):
            for t in range(n_tp):
                pl.semaphore_signal(barrier, inc=1, device_id=at(s, t, 0), device_id_type=MESH)
        for k in range(1, n_tp):
            pl.semaphore_signal(
                barrier, inc=1, device_id=at(seq, lax.rem(tp + k, n_tp), 1), device_id_type=MESH
            )
        for load in loads:
            load.wait()
        pool_copy.wait()
        most = table_ref.shape[2]
        tokens = lax.broadcasted_iota(jnp.int32, (1, most * page), 1)
        for r in range(rows):
            keys = jnp.concatenate([pool[table_ref[r, 0, j]] for j in range(most)], axis=1)
            scores = jnp.dot(q_ref[r], keys, preferred_element_type=jnp.float32) * SOFT_SCALE
            live = tokens < res_ref[0, r]
            scores = jnp.where(live, scores, MASKED)
            row_max = jnp.max(scores, axis=1, keepdims=True)
            e = jnp.where(live, jnp.exp(scores - row_max), 0.0)
            row_total = jnp.sum(e, axis=1, keepdims=True)
            part_out = lax.dot_general(
                e.astype(jnp.bfloat16), keys[:latent],
                (((1,), (1,)), ((), ())), preferred_element_type=jnp.float32,
            )
            for t in range(n_tp):
                mine = slice(t * share, (t + 1) * share)
                for c in range(chunks):
                    res_out[t, r, c * share : (c + 1) * share] = part_out[
                        mine, c * 128 : (c + 1) * 128
                    ]
                res_out[t, r, chunks * share :, :share] = stats_rows(
                    row_max[mine], row_total[mine], 0.0
                )
        if n_tp > 1:
            pl.semaphore_wait(barrier, n_tp - 1)
        for k in range(1, n_tp):
            res_copy(lax.rem(tp + k, n_tp), tp).start()
        res_in[tp] = res_out[tp]
        for k in range(1, n_tp):
            peer = lax.rem(tp + k, n_tp)
            res_copy(peer, peer).wait_recv()

        def columns(block):
            wide = jnp.concatenate([block[:, :share], jnp.zeros((8, 128 - share))], axis=1)
            turned = wide.T
            return turned[:share, 0:1], turned[:share, 1:2], turned[:share, 2:3]

        def joined(block, scale, sums):
            return [
                sums[c] + block[c * share : (c + 1) * share] * scale for c in range(chunks)
            ]

        tail = slice(chunks * share, chunks * share + 8)
        resident = []
        for r in range(rows):
            parts = [columns(res_in[t, r, tail]) for t in range(n_tp)]
            joint = functools.reduce(jnp.maximum, [part[0] for part in parts])
            total = jnp.zeros((share, 1), jnp.float32)
            sums = [jnp.zeros((share, 128), jnp.float32)] * chunks
            for t in range(n_tp):
                scale = jnp.exp(parts[t][0] - joint)
                total += parts[t][1] * scale
                sums = joined(res_in[t, r], scale, sums)
            for c in range(chunks):
                res_sum[r, c * share : (c + 1) * share] = sums[c]
            resident.append((joint, total))
        for p in range(n_seq * n_tp):
            piece_copy(0, 0, p).wait_recv()
        pieces = [columns(piece_in[p, tail]) for p in range(n_seq * n_tp)]
        for r in range(rows):
            row_max, row_total = resident[r]
            maxima = [
                jnp.where(slot == float(r), piece_max, MASKED) for piece_max, _, slot in pieces
            ]
            joint = functools.reduce(jnp.maximum, maxima, row_max)
            scale = jnp.exp(row_max - joint)
            total = row_total * scale
            sums = [res_sum[r, c * share : (c + 1) * share] * scale for c in range(chunks)]
            for p in range(n_seq * n_tp):
                scale = jnp.where(
                    pieces[p][2] == float(r), jnp.exp(maxima[p] - joint), 0.0
                )
                total += pieces[p][1] * scale
                sums = joined(piece_in[p], scale, sums)
            for c in range(chunks):
                out_ref[0, r, :, c * 128 : (c + 1) * 128] = (sums[c] / total).astype(jnp.bfloat16)
        for k in range(1, n_tp):
            res_copy(lax.rem(tp + k, n_tp), tp).wait_send()


def local(
    n_seq, n_tp,
    page_pool, queries, block_table, res_len, piece_len, piece_owner, piece_slot, piece_pos, kv_gain
):
    pages, page, width = page_pool.shape
    rows, heads, _ = queries.shape
    latent = kv_gain.shape[0]
    share = heads // n_tp
    packed = latent // 128 * share + 8
    vmem = pl.BlockSpec(memory_space=pltpu.VMEM)
    parts = n_seq * n_tp
    return pl.pallas_call(
        functools.partial(kernel, n_seq, n_tp),
        out_shape=jax.ShapeDtypeStruct((1, rows, share, latent), jnp.bfloat16),
        in_specs=[pl.BlockSpec(memory_space=pl.ANY)] * 9,
        out_specs=vmem,
        scratch_shapes=[
            pltpu.VMEM(queries.shape, jnp.bfloat16),
            pltpu.SMEM(block_table.shape, jnp.int32),
            pltpu.SMEM(res_len.shape[::-1], jnp.int32),
            pltpu.SMEM(piece_len.shape, jnp.int32),
            pltpu.SMEM(piece_len.shape, jnp.int32),
            pltpu.SMEM(piece_len.shape, jnp.int32),
            pltpu.SMEM(piece_len.shape, jnp.int32),
            pltpu.VMEM((1, latent), jnp.float32),
            pltpu.SemaphoreType.DMA((8,)),
            pltpu.VMEM((pages, width, page), jnp.bfloat16),
            pltpu.VMEM((width, FRESH_DEV), jnp.bfloat16),
            pltpu.VMEM((n_seq, heads, width), jnp.bfloat16),
            pltpu.VMEM((n_seq, heads, width), jnp.bfloat16),
            pltpu.VMEM((n_seq, 8, 128), jnp.int32),
            pltpu.VMEM((n_seq, 8, 128), jnp.int32),
            pltpu.VMEM((n_seq, n_tp, packed, 128), jnp.float32),
            pltpu.VMEM((parts, packed, 128), jnp.float32),
            pltpu.VMEM((n_tp, rows, packed, 128), jnp.float32),
            pltpu.VMEM((n_tp, rows, packed, 128), jnp.float32),
            pltpu.VMEM((rows, packed, 128), jnp.float32),
            pltpu.SemaphoreType.DMA,
            pltpu.SemaphoreType.DMA((n_seq,)),
            pltpu.SemaphoreType.DMA((n_seq,)),
            pltpu.SemaphoreType.DMA((n_seq,)),
            pltpu.SemaphoreType.DMA((n_seq,)),
            pltpu.SemaphoreType.DMA((parts,)),
            pltpu.SemaphoreType.DMA((parts,)),
            pltpu.SemaphoreType.DMA((n_tp,)),
            pltpu.SemaphoreType.DMA((n_tp,)),
        ],
        compiler_params=pltpu.CompilerParams(
            collective_id=0, has_side_effects=True, vmem_limit_bytes=56 * 1024 * 1024
        ),
    )(
        jnp.swapaxes(page_pool, 1, 2), queries, block_table, res_len.T, piece_len,
        piece_owner, piece_slot, piece_pos, kv_gain[None],
    )


def solution(mesh):
    return jax.shard_map(
        functools.partial(local, mesh.shape["seq"], mesh.shape["tp"]),
        mesh=mesh,
        in_specs=(
            P(("groups", "seq", "tp", "section"), None, None),
            P(("groups", "seq"), None, None),
            P(("groups", "seq"), "tp", None),
            P(("groups", "seq"), "tp"),
            P(("groups", "seq"), "tp", None),
            P(("groups", "seq"), "tp", None),
            P(("groups", "seq"), "tp", None),
            P(("groups", "seq"), "tp", None),
            P(),
        ),
        out_specs=P("section", ("groups", "seq"), "tp", None),
        check_vma=False,
    )
```

```python
import functools

import jax
import jax.numpy as jnp
import numpy as np
from jax import lax
from jax.experimental import pallas as pl
from jax.experimental.pallas import tpu as pltpu
from jax.sharding import PartitionSpec as P

FRESH_DEV = 1024
SOFT_SCALE = 192.0 ** (-0.5)
MASKED = -1e30
NORM_EPSILON = 1e-06
GROUP = 2
STEPS = 32700.0
MESH = pl.DeviceIdType.MESH


def stats_rows(row_max, row_total, slot, step):
    lane = lax.broadcasted_iota(jnp.int32, (row_max.shape[0], 128), 1)
    block = jnp.where(
        lane == 0, row_max, jnp.where(lane == 1, row_total, jnp.where(lane == 2, slot, step))
    )
    return block.T[:8]


def cos_sin(angles):
    turns = jnp.floor(angles * (2.0 / np.pi) + 0.5)
    rest = angles - turns * 1.5703125
    rest = rest - turns * 4.837512969970703125e-4
    rest = rest - turns * 7.54978995489188216e-8
    square = rest * rest
    sine = rest + rest * square * (
        -1.6666654611e-1 + square * (8.3321608736e-3 + square * -1.9515295891e-4)
    )
    cosine = (
        1.0
        - 0.5 * square
        + square * square
        * (4.166664568298827e-2 + square * (-1.388731625493765e-3 + square * 2.443315711809948e-5))
    )
    quarter = turns.astype(jnp.int32) & 3
    odd = (quarter & 1) == 1
    cos_value = jnp.where(odd, sine, cosine)
    sin_value = jnp.where(odd, cosine, sine)
    cos_value = jnp.where((quarter == 1) | (quarter == 2), -cos_value, cos_value)
    sin_value = jnp.where(quarter >= 2, -sin_value, sin_value)
    return cos_value, sin_value


def kernel(
    n_seq, n_tp, pool_hbm, q_hbm, table_hbm, res_hbm, len_hbm, owner_hbm, slot_hbm, pos_hbm,
    gain_hbm, out_ref,
    q_ref, table_ref, res_ref, len_ref, owner_ref, slot_ref, pos_ref, gain_ref, load_sem,
    pool, fresh, q_in, q_out, meta_in, meta_out, piece_out, piece_in, stat_out, stat_in, scales, res_out, res_in, res_sum,
    pool_sem, meta_send, meta_recv, q_send, q_recv, piece_send, piece_recv, stat_send, stat_recv,
    res_send, res_recv,
):
    pages, width, page = pool.shape
    rows, heads, _ = q_ref.shape
    latent = gain_ref.shape[1]
    half = (width - latent) // 2
    share = heads // n_tp
    fresh_pages = FRESH_DEV // page
    chunks = latent // 128
    seq = lax.axis_index("seq")
    tp = lax.axis_index("tp")
    section = lax.axis_index("section")
    barrier = pltpu.get_barrier_semaphore()
    order = [lax.rem((seq // 2) * 2 + 2 + i, n_seq) for i in range(n_seq)]
    peers = order[: n_seq - 2] + [(seq // 2) * 2 + 1 - lax.rem(seq, 2)]

    loads = [
        pltpu.make_async_copy(source, target, load_sem.at[i])
        for i, (source, target) in enumerate(
            [
                (len_hbm, len_ref), (owner_hbm, owner_ref), (slot_hbm, slot_ref),
                (pos_hbm, pos_ref), (table_hbm, table_ref), (res_hbm, res_ref),
                (q_hbm, q_ref), (gain_hbm, gain_ref),
            ]
        )
    ]
    for load in loads:
        load.start()

    def at(s, t, c):
        return {"seq": s, "tp": t, "section": c}

    def meta_copy(peer, own):
        return pltpu.make_async_remote_copy(
            meta_out.at[peer], meta_in.at[own], meta_send.at[peer], meta_recv.at[own],
            device_id=at(peer, tp, 0), device_id_type=MESH,
        )

    def q_copy(peer, own):
        return pltpu.make_async_remote_copy(
            q_out.at[peer], q_in.at[own], q_send.at[peer], q_recv.at[own],
            device_id=at(peer, tp, 0), device_id_type=MESH,
        )

    def piece_copy(i, t, own):
        return pltpu.make_async_remote_copy(
            piece_out.at[i, t], piece_in.at[own], piece_send.at[i * n_tp + t], piece_recv.at[own],
            device_id=at(order[i], t, 1), device_id_type=MESH,
        )

    def stat_copy(i, t, own):
        return pltpu.make_async_remote_copy(
            stat_out.at[i, t], stat_in.at[own], stat_send.at[i * n_tp + t], stat_recv.at[own],
            device_id=at(order[i], t, 1), device_id_type=MESH,
        )

    def res_copy(t, own):
        return pltpu.make_async_remote_copy(
            res_out.at[t], res_in.at[own], res_send.at[t], res_recv.at[own],
            device_id=at(seq, t, 1), device_id_type=MESH,
        )

    @pl.when(section == 0)
    def prefill():
        raw_copy = pltpu.make_async_copy(
            pool_hbm.at[pl.ds(0, fresh_pages)], pool.at[pl.ds(0, fresh_pages)], pool_sem
        )
        raw_copy.start()
        for peer in peers:
            pl.semaphore_signal(barrier, inc=1, device_id=at(peer, tp, 0), device_id_type=MESH)
        for load in loads:
            load.wait()

        lengths = [len_ref[0, 0, k] for k in range(n_seq)]
        begins = [jnp.int32(0)]
        for k in range(n_seq - 1):
            begins.append(begins[-1] + lengths[k])

        def of_owner(d, values):
            total = jnp.int32(0)
            for k in range(n_seq):
                total = total + jnp.where(owner_ref[0, 0, k] == d, values[k], 0)
            return total

        slots = [slot_ref[0, 0, k] for k in range(n_seq)]
        owner_begin = [of_owner(d, begins) for d in order]
        owner_len = [of_owner(d, lengths) for d in order]
        owner_slot = [of_owner(d, slots) for d in order]
        for i, d in enumerate(order):
            meta_out[d] = jnp.full(meta_out.shape[1:], owner_slot[i], jnp.int32)

        pl.semaphore_wait(barrier, n_seq - 1 + n_seq * n_tp)
        for peer in peers:
            meta_copy(peer, seq).start()

        for peer in peers:
            meta_copy(peer, peer).wait_recv()
            wanted = meta_in[peer][0:1, 0:1]
            picked = q_ref[0].astype(jnp.float32)
            for r in range(1, rows):
                picked = jnp.where(wanted == r, q_ref[r].astype(jnp.float32), picked)
            q_out[peer] = picked.astype(jnp.bfloat16)
            q_copy(peer, seq).start()
        own_slot = meta_out[seq][0:1, 0:1]
        picked = q_ref[0].astype(jnp.float32)
        for r in range(1, rows):
            picked = jnp.where(own_slot == r, q_ref[r].astype(jnp.float32), picked)
        q_in[seq] = picked.astype(jnp.bfloat16)

        out_ref[...] = jnp.zeros_like(out_ref)
        raw_copy.wait()
        gain = jnp.broadcast_to(gain_ref[...], (page, latent)).T
        index = lax.broadcasted_iota(jnp.int32, (half, page), 0)
        freq = jnp.ones((half, page), jnp.float32)
        for i in range(1, half):
            freq = jnp.where(index == i, float(10000.0 ** (-i / half)), freq)
        for j in range(fresh_pages):
            x = pool[j, :latent].astype(jnp.float32)
            mean = jnp.mean(x * x, axis=0, keepdims=True)
            columns = slice(j * page, (j + 1) * page)
            normed = x * lax.rsqrt(mean + NORM_EPSILON) * gain
            fresh[:latent, columns] = normed.astype(jnp.bfloat16)
            y = pool[j, latent:].astype(jnp.float32)
            a, b = y[:half], y[half:]
            token = lax.broadcasted_iota(jnp.int32, (1, page), 1) + j * page
            shift = jnp.zeros((1, page), jnp.int32)
            for k in range(n_seq):
                live = (token >= begins[k]) & (token < begins[k] + lengths[k])
                shift = jnp.where(live, pos_ref[0, 0, k] - begins[k], shift)
            cosine, sine = cos_sin((token + shift).astype(jnp.float32) * freq)
            turned = jnp.concatenate([a * cosine - b * sine, b * cosine + a * sine], axis=0)
            fresh[latent:, columns] = turned.astype(jnp.bfloat16)

        out_ref[...] = jnp.zeros_like(out_ref)
        tokens = lax.broadcasted_iota(jnp.int32, (1, FRESH_DEV), 1)
        for first in range(0, n_seq, GROUP):
            for d in peers[first : first + GROUP]:
                q_copy(d, d).wait_recv()
            members = range(first, first + GROUP)
            wide = jnp.concatenate([q_in[order[i]] for i in members], axis=0)
            scores = jnp.dot(wide, fresh[...], preferred_element_type=jnp.float32) * SOFT_SCALE
            stats = []
            weights = []
            for i in members:
                live = (tokens >= owner_begin[i]) & (tokens < owner_begin[i] + owner_len[i])
                here = (i - first) * heads
                part = jnp.where(live, scores[here : here + heads], MASKED)
                row_max = jnp.max(part, axis=1, keepdims=True)
                e = jnp.where(live, jnp.exp(part - row_max), 0.0)
                row_total = jnp.sum(e, axis=1, keepdims=True)
                weights.append(e.astype(jnp.bfloat16))
                stats.append((row_max, row_total, owner_slot[i].astype(jnp.float32)))
            group_out = lax.dot_general(
                jnp.concatenate(weights, axis=0), fresh[:latent],
                (((1,), (1,)), ((), ())), preferred_element_type=jnp.float32,
            )
            step = jnp.maximum(jnp.max(jnp.abs(group_out), axis=1, keepdims=True), 1e-30) / STEPS
            for i in members:
                row_max, row_total, slot = stats[i - first]
                here = (i - first) * heads
                for t in range(n_tp):
                    mine = slice(t * share, (t + 1) * share)
                    stat_out[i, t, :, :share] = stats_rows(
                        row_max[mine], row_total[mine], slot,
                        step[here + t * share : here + (t + 1) * share],
                    )
                    stat_copy(i, t, seq * n_tp + tp).start()
            counted = jnp.floor(group_out * (1.0 / step) + 0.5)
            for i in members:
                for t in range(n_tp):
                    here = (i - first) * heads + t * share
                    stacked = jnp.concatenate(
                        [
                            counted[here : here + share, c * 128 : (c + 1) * 128]
                            for c in range(chunks)
                        ],
                        axis=0,
                    )
                    piece_out[i, t] = stacked.astype(jnp.int32).astype(jnp.int16)
                    piece_copy(i, t, seq * n_tp + tp).start()

        for peer in peers:
            meta_copy(peer, peer).wait_send()
            q_copy(peer, peer).wait_send()
        for d in range(n_seq):
            for t in range(n_tp):
                piece_copy(d, t, 0).wait_send()
                stat_copy(d, t, 0).wait_send()

    @pl.when(section == 1)
    def decode():
        pool_copy = pltpu.make_async_copy(pool_hbm, pool, pool_sem)
        pool_copy.start()
        for s in range(n_seq):
            for t in range(n_tp):
                pl.semaphore_signal(barrier, inc=1, device_id=at(s, t, 0), device_id_type=MESH)
        for k in range(1, n_tp):
            pl.semaphore_signal(
                barrier, inc=1, device_id=at(seq, lax.rem(tp + k, n_tp), 1), device_id_type=MESH
            )
        for load in loads:
            load.wait()
        pool_copy.wait()
        most = table_ref.shape[2]
        tokens = lax.broadcasted_iota(jnp.int32, (1, most * page), 1)
        for r in range(rows):
            keys = jnp.concatenate([pool[table_ref[r, 0, j]] for j in range(most)], axis=1)
            scores = jnp.dot(q_ref[r], keys, preferred_element_type=jnp.float32) * SOFT_SCALE
            live = tokens < res_ref[0, r]
            scores = jnp.where(live, scores, MASKED)
            row_max = jnp.max(scores, axis=1, keepdims=True)
            e = jnp.where(live, jnp.exp(scores - row_max), 0.0)
            row_total = jnp.sum(e, axis=1, keepdims=True)
            part_out = lax.dot_general(
                e.astype(jnp.bfloat16), keys[:latent],
                (((1,), (1,)), ((), ())), preferred_element_type=jnp.float32,
            )
            for t in range(n_tp):
                mine = slice(t * share, (t + 1) * share)
                for c in range(chunks):
                    res_out[t, r, c * share : (c + 1) * share] = part_out[
                        mine, c * 128 : (c + 1) * 128
                    ]
                res_out[t, r, chunks * share :, :share] = stats_rows(
                    row_max[mine], row_total[mine], 0.0, 0.0
                )
        if n_tp > 1:
            pl.semaphore_wait(barrier, n_tp - 1)
        for k in range(1, n_tp):
            res_copy(lax.rem(tp + k, n_tp), tp).start()
        res_in[tp] = res_out[tp]
        for k in range(1, n_tp):
            peer = lax.rem(tp + k, n_tp)
            res_copy(peer, peer).wait_recv()

        def columns(block):
            wide = jnp.concatenate([block[:, :share], jnp.zeros((8, 128 - share))], axis=1)
            turned = wide.T
            return [turned[:share, i : i + 1] for i in range(4)]

        def joined(block, scale, sums):
            return [
                sums[c] + block[c * share : (c + 1) * share] * scale for c in range(chunks)
            ]

        tail = slice(chunks * share, chunks * share + 8)
        resident = []
        for r in range(rows):
            parts = [columns(res_in[t, r, tail]) for t in range(n_tp)]
            joint = functools.reduce(jnp.maximum, [part[0] for part in parts])
            total = jnp.zeros((share, 1), jnp.float32)
            sums = [jnp.zeros((share, 128), jnp.float32)] * chunks
            for t in range(n_tp):
                scale = jnp.exp(parts[t][0] - joint)
                total += parts[t][1] * scale
                sums = joined(res_in[t, r], scale, sums)
            for c in range(chunks):
                res_sum[r, c * share : (c + 1) * share] = sums[c]
            resident.append((joint, total))
        for p in range(n_seq * n_tp):
            stat_copy(0, 0, p).wait_recv()
        pieces = [columns(stat_in[p]) for p in range(n_seq * n_tp)]
        for r in range(rows):
            row_max, row_total = resident[r]
            maxima = [
                jnp.where(slot == float(r), piece_max, MASKED) for piece_max, _, slot, _ in pieces
            ]
            joint = functools.reduce(jnp.maximum, maxima, row_max)
            factor = jnp.exp(row_max - joint)
            factors = [
                jnp.where(pieces[p][2] == float(r), jnp.exp(maxima[p] - joint), 0.0)
                for p in range(n_seq * n_tp)
            ]
            total = row_total * factor
            for p in range(n_seq * n_tp):
                total += pieces[p][1] * factors[p]
            inverse = 1.0 / total
            for p in range(n_seq * n_tp):
                scales[r, p] = jnp.broadcast_to(factors[p] * pieces[p][3] * inverse, (share, 128))
            for c in range(chunks):
                block = slice(c * share, (c + 1) * share)
                res_sum[r, block] = res_sum[r, block] * (factor * inverse)
        for p in range(n_seq * n_tp):
            piece_copy(0, 0, p).wait_recv()
        for c in range(chunks):
            block = slice(c * share, (c + 1) * share)
            sums = [res_sum[r, block] for r in range(rows)]
            for p in range(n_seq * n_tp):
                value = piece_in[p][block].astype(jnp.int32).astype(jnp.float32)
                sums = [sums[r] + value * scales[r, p] for r in range(rows)]
            for r in range(rows):
                out_ref[0, r, :, c * 128 : (c + 1) * 128] = sums[r].astype(out_ref.dtype)
        for k in range(1, n_tp):
            res_copy(lax.rem(tp + k, n_tp), tp).wait_send()


def local(
    n_seq, n_tp,
    page_pool, queries, block_table, res_len, piece_len, piece_owner, piece_slot, piece_pos, kv_gain
):
    pages, page, width = page_pool.shape
    rows, heads, _ = queries.shape
    latent = kv_gain.shape[0]
    share = heads // n_tp
    packed = latent // 128 * share + 8
    vmem = pl.BlockSpec(memory_space=pltpu.VMEM)
    parts = n_seq * n_tp
    return pl.pallas_call(
        functools.partial(kernel, n_seq, n_tp),
        out_shape=jax.ShapeDtypeStruct((1, rows, share, latent), jnp.float32),
        in_specs=[pl.BlockSpec(memory_space=pl.ANY)] * 9,
        out_specs=vmem,
        scratch_shapes=[
            pltpu.VMEM(queries.shape, jnp.bfloat16),
            pltpu.SMEM(block_table.shape, jnp.int32),
            pltpu.SMEM(res_len.shape[::-1], jnp.int32),
            pltpu.SMEM(piece_len.shape, jnp.int32),
            pltpu.SMEM(piece_len.shape, jnp.int32),
            pltpu.SMEM(piece_len.shape, jnp.int32),
            pltpu.SMEM(piece_len.shape, jnp.int32),
            pltpu.VMEM((1, latent), jnp.float32),
            pltpu.SemaphoreType.DMA((8,)),
            pltpu.VMEM((pages, width, page), jnp.bfloat16),
            pltpu.VMEM((width, FRESH_DEV), jnp.bfloat16),
            pltpu.VMEM((n_seq, heads, width), jnp.bfloat16),
            pltpu.VMEM((n_seq, heads, width), jnp.bfloat16),
            pltpu.VMEM((n_seq, 8, 128), jnp.int32),
            pltpu.VMEM((n_seq, 8, 128), jnp.int32),
            pltpu.VMEM((n_seq, n_tp, packed - 8, 128), jnp.int16),
            pltpu.VMEM((parts, packed - 8, 128), jnp.int16),
            pltpu.VMEM((n_seq, n_tp, 8, 128), jnp.float32),
            pltpu.VMEM((parts, 8, 128), jnp.float32),
            pltpu.VMEM((rows, parts, share, 128), jnp.float32),
            pltpu.VMEM((n_tp, rows, packed, 128), jnp.float32),
            pltpu.VMEM((n_tp, rows, packed, 128), jnp.float32),
            pltpu.VMEM((rows, packed, 128), jnp.float32),
            pltpu.SemaphoreType.DMA,
            pltpu.SemaphoreType.DMA((n_seq,)),
            pltpu.SemaphoreType.DMA((n_seq,)),
            pltpu.SemaphoreType.DMA((n_seq,)),
            pltpu.SemaphoreType.DMA((n_seq,)),
            pltpu.SemaphoreType.DMA((parts,)),
            pltpu.SemaphoreType.DMA((parts,)),
            pltpu.SemaphoreType.DMA((parts,)),
            pltpu.SemaphoreType.DMA((parts,)),
            pltpu.SemaphoreType.DMA((n_tp,)),
            pltpu.SemaphoreType.DMA((n_tp,)),
        ],
        compiler_params=pltpu.CompilerParams(
            collective_id=0, has_side_effects=True, vmem_limit_bytes=56 * 1024 * 1024
        ),
    )(
        jnp.swapaxes(page_pool, 1, 2), queries, block_table, res_len.T, piece_len,
        piece_owner, piece_slot, piece_pos, kv_gain[None],
    ).astype(jnp.bfloat16)


def solution(mesh):
    return jax.shard_map(
        functools.partial(local, mesh.shape["seq"], mesh.shape["tp"]),
        mesh=mesh,
        in_specs=(
            P(("groups", "seq", "tp", "section"), None, None),
            P(("groups", "seq"), None, None),
            P(("groups", "seq"), "tp", None),
            P(("groups", "seq"), "tp"),
            P(("groups", "seq"), "tp", None),
            P(("groups", "seq"), "tp", None),
            P(("groups", "seq"), "tp", None),
            P(("groups", "seq"), "tp", None),
            P(),
        ),
        out_specs=P("section", ("groups", "seq"), "tp", None),
        check_vma=False,
    )
```

```python
import functools

import jax
import jax.numpy as jnp
import numpy as np
from jax import lax
from jax.experimental import pallas as pl
from jax.experimental.pallas import tpu as pltpu
from jax.sharding import PartitionSpec as P

FRESH_DEV = 1024
SOFT_SCALE = 192.0 ** (-0.5)
MASKED = -1e30
NORM_EPSILON = 1e-06
GROUP = 2
STEPS = 32700.0
MESH = pl.DeviceIdType.MESH


def stats_rows(row_max, row_total, slot, step):
    lane = lax.broadcasted_iota(jnp.int32, (row_max.shape[0], 128), 1)
    block = jnp.where(
        lane == 0, row_max, jnp.where(lane == 1, row_total, jnp.where(lane == 2, slot, step))
    )
    return block.T[:8]


def cos_sin(angles):
    turns = jnp.floor(angles * (2.0 / np.pi) + 0.5)
    rest = angles - turns * 1.5703125
    rest = rest - turns * 4.837512969970703125e-4
    rest = rest - turns * 7.54978995489188216e-8
    square = rest * rest
    sine = rest + rest * square * (
        -1.6666654611e-1 + square * (8.3321608736e-3 + square * -1.9515295891e-4)
    )
    cosine = (
        1.0
        - 0.5 * square
        + square * square
        * (4.166664568298827e-2 + square * (-1.388731625493765e-3 + square * 2.443315711809948e-5))
    )
    quarter = turns.astype(jnp.int32) & 3
    odd = (quarter & 1) == 1
    cos_value = jnp.where(odd, sine, cosine)
    sin_value = jnp.where(odd, cosine, sine)
    cos_value = jnp.where((quarter == 1) | (quarter == 2), -cos_value, cos_value)
    sin_value = jnp.where(quarter >= 2, -sin_value, sin_value)
    return cos_value, sin_value


def kernel(
    n_seq, n_tp, pool_hbm, q_hbm, table_hbm, res_hbm, len_hbm, owner_hbm, slot_hbm, pos_hbm,
    gain_hbm, out_ref,
    q_ref, table_ref, res_ref, len_ref, owner_ref, slot_ref, pos_ref, gain_ref, load_sem,
    pool, fresh, q_in, q_out, meta_in, meta_out, piece_out, piece_in, stat_out, stat_in, scales, res_out, res_in, res_sum,
    pool_sem, meta_send, meta_recv, q_send, q_recv, piece_send, piece_recv, stat_send, stat_recv,
    res_send, res_recv,
):
    pages, width, page = pool.shape
    rows, heads, _ = q_ref.shape
    latent = gain_ref.shape[1]
    half = (width - latent) // 2
    share = heads // n_tp
    fresh_pages = FRESH_DEV // page
    chunks = latent // 128
    seq = lax.axis_index("seq")
    tp = lax.axis_index("tp")
    section = lax.axis_index("section")
    barrier = pltpu.get_barrier_semaphore()
    order = [lax.rem((seq // 2) * 2 + i, n_seq) for i in range(n_seq)]
    peers = [(seq // 2) * 2 + 1 - lax.rem(seq, 2)] + order[2:]

    loads = [
        pltpu.make_async_copy(source, target, load_sem.at[i])
        for i, (source, target) in enumerate(
            [
                (len_hbm, len_ref), (owner_hbm, owner_ref), (slot_hbm, slot_ref),
                (pos_hbm, pos_ref), (table_hbm, table_ref), (res_hbm, res_ref),
                (q_hbm, q_ref), (gain_hbm, gain_ref),
            ]
        )
    ]
    def at(s, t, c):
        return {"seq": s, "tp": t, "section": c}

    def meta_copy(peer, own):
        return pltpu.make_async_remote_copy(
            meta_out.at[peer], meta_in.at[own], meta_send.at[peer], meta_recv.at[own],
            device_id=at(peer, tp, 0), device_id_type=MESH,
        )

    def q_copy(peer, own):
        return pltpu.make_async_remote_copy(
            q_out.at[peer], q_in.at[own], q_send.at[peer], q_recv.at[own],
            device_id=at(peer, tp, 0), device_id_type=MESH,
        )

    def piece_copy(i, t, own):
        return pltpu.make_async_remote_copy(
            piece_out.at[i, t], piece_in.at[own], piece_send.at[i * n_tp + t], piece_recv.at[own],
            device_id=at(order[i], t, 1), device_id_type=MESH,
        )

    def stat_copy(i, t, own):
        return pltpu.make_async_remote_copy(
            stat_out.at[i, t], stat_in.at[own], stat_send.at[i * n_tp + t], stat_recv.at[own],
            device_id=at(order[i], t, 1), device_id_type=MESH,
        )

    def res_copy(t, own):
        return pltpu.make_async_remote_copy(
            res_out.at[t], res_in.at[own], res_send.at[t], res_recv.at[own],
            device_id=at(seq, t, 1), device_id_type=MESH,
        )

    @pl.when(section == 0)
    def prefill():
        raw_copy = pltpu.make_async_copy(
            pool_hbm.at[pl.ds(0, fresh_pages)], pool.at[pl.ds(0, fresh_pages)], pool_sem
        )
        for peer in peers:
            pl.semaphore_signal(barrier, inc=1, device_id=at(peer, tp, 0), device_id_type=MESH)
        for load in loads:
            load.start()
        raw_copy.start()
        for load in loads:
            load.wait()

        lengths = [len_ref[0, 0, k] for k in range(n_seq)]
        begins = [jnp.int32(0)]
        for k in range(n_seq - 1):
            begins.append(begins[-1] + lengths[k])

        def of_owner(d, values):
            total = jnp.int32(0)
            for k in range(n_seq):
                total = total + jnp.where(owner_ref[0, 0, k] == d, values[k], 0)
            return total

        slots = [slot_ref[0, 0, k] for k in range(n_seq)]
        owner_begin = [of_owner(d, begins) for d in order]
        owner_len = [of_owner(d, lengths) for d in order]
        owner_slot = [of_owner(d, slots) for d in order]
        for i, d in enumerate(order):
            meta_out[d] = jnp.full(meta_out.shape[1:], owner_slot[i], jnp.int32)

        pl.semaphore_wait(barrier, n_seq - 1 + n_seq * n_tp)
        for peer in peers:
            meta_copy(peer, seq).start()

        for peer in peers:
            meta_copy(peer, peer).wait_recv()
            wanted = meta_in[peer][0:1, 0:1]
            picked = q_ref[0].astype(jnp.float32)
            for r in range(1, rows):
                picked = jnp.where(wanted == r, q_ref[r].astype(jnp.float32), picked)
            q_out[peer] = picked.astype(jnp.bfloat16)
            q_copy(peer, seq).start()
        own_slot = meta_out[seq][0:1, 0:1]
        picked = q_ref[0].astype(jnp.float32)
        for r in range(1, rows):
            picked = jnp.where(own_slot == r, q_ref[r].astype(jnp.float32), picked)
        q_in[seq] = picked.astype(jnp.bfloat16)

        out_ref[...] = jnp.zeros_like(out_ref)
        raw_copy.wait()
        gain = jnp.broadcast_to(gain_ref[...], (page, latent)).T
        index = lax.broadcasted_iota(jnp.int32, (half, page), 0)
        freq = jnp.ones((half, page), jnp.float32)
        for i in range(1, half):
            freq = jnp.where(index == i, float(10000.0 ** (-i / half)), freq)
        for j in range(fresh_pages):
            x = pool[j, :latent].astype(jnp.float32)
            mean = jnp.mean(x * x, axis=0, keepdims=True)
            columns = slice(j * page, (j + 1) * page)
            normed = x * lax.rsqrt(mean + NORM_EPSILON) * gain
            fresh[:latent, columns] = normed.astype(jnp.bfloat16)
            y = pool[j, latent:].astype(jnp.float32)
            a, b = y[:half], y[half:]
            token = lax.broadcasted_iota(jnp.int32, (1, page), 1) + j * page
            shift = jnp.zeros((1, page), jnp.int32)
            for k in range(n_seq):
                live = (token >= begins[k]) & (token < begins[k] + lengths[k])
                shift = jnp.where(live, pos_ref[0, 0, k] - begins[k], shift)
            cosine, sine = cos_sin((token + shift).astype(jnp.float32) * freq)
            turned = jnp.concatenate([a * cosine - b * sine, b * cosine + a * sine], axis=0)
            fresh[latent:, columns] = turned.astype(jnp.bfloat16)

        out_ref[...] = jnp.zeros_like(out_ref)
        tokens = lax.broadcasted_iota(jnp.int32, (1, FRESH_DEV), 1)
        for first in range(0, n_seq, GROUP):
            for d in peers[max(first - 1, 0) : first + GROUP - 1]:
                q_copy(d, d).wait_recv()
            members = range(first, first + GROUP)
            wide = jnp.concatenate([q_in[order[i]] for i in members], axis=0)
            scores = jnp.dot(wide, fresh[...], preferred_element_type=jnp.float32) * SOFT_SCALE
            stats = []
            weights = []
            for i in members:
                live = (tokens >= owner_begin[i]) & (tokens < owner_begin[i] + owner_len[i])
                here = (i - first) * heads
                part = jnp.where(live, scores[here : here + heads], MASKED)
                row_max = jnp.max(part, axis=1, keepdims=True)
                e = jnp.where(live, jnp.exp(part - row_max), 0.0)
                row_total = jnp.sum(e, axis=1, keepdims=True)
                weights.append(e.astype(jnp.bfloat16))
                stats.append((row_max, row_total, owner_slot[i].astype(jnp.float32)))
            group_out = lax.dot_general(
                jnp.concatenate(weights, axis=0), fresh[:latent],
                (((1,), (1,)), ((), ())), preferred_element_type=jnp.float32,
            )
            step = jnp.maximum(jnp.max(jnp.abs(group_out), axis=1, keepdims=True), 1e-30) / STEPS
            for i in members:
                row_max, row_total, slot = stats[i - first]
                here = (i - first) * heads
                for t in range(n_tp):
                    mine = slice(t * share, (t + 1) * share)
                    stat_out[i, t, :, :share] = stats_rows(
                        row_max[mine], row_total[mine], slot,
                        step[here + t * share : here + (t + 1) * share],
                    )
                    stat_copy(i, t, seq * n_tp + tp).start()
            counted = jnp.floor(group_out * (1.0 / step) + 0.5)
            for i in members:
                for t in range(n_tp):
                    here = (i - first) * heads + t * share
                    stacked = jnp.concatenate(
                        [
                            counted[here : here + share, c * 128 : (c + 1) * 128]
                            for c in range(chunks)
                        ],
                        axis=0,
                    )
                    piece_out[i, t] = stacked.astype(jnp.int32).astype(jnp.int16)
                    piece_copy(i, t, seq * n_tp + tp).start()

        for peer in peers:
            meta_copy(peer, peer).wait_send()
            q_copy(peer, peer).wait_send()
        for d in range(n_seq):
            for t in range(n_tp):
                piece_copy(d, t, 0).wait_send()
                stat_copy(d, t, 0).wait_send()

    @pl.when(section == 1)
    def decode():
        pool_copy = pltpu.make_async_copy(pool_hbm, pool, pool_sem)
        for s in range(n_seq):
            for t in range(n_tp):
                pl.semaphore_signal(barrier, inc=1, device_id=at(s, t, 0), device_id_type=MESH)
        for k in range(1, n_tp):
            pl.semaphore_signal(
                barrier, inc=1, device_id=at(seq, lax.rem(tp + k, n_tp), 1), device_id_type=MESH
            )
        for load in loads:
            load.start()
        pool_copy.start()
        for load in loads:
            load.wait()
        pool_copy.wait()
        most = table_ref.shape[2]
        tokens = lax.broadcasted_iota(jnp.int32, (1, most * page), 1)
        for r in range(rows):
            keys = jnp.concatenate([pool[table_ref[r, 0, j]] for j in range(most)], axis=1)
            scores = jnp.dot(q_ref[r], keys, preferred_element_type=jnp.float32) * SOFT_SCALE
            live = tokens < res_ref[0, r]
            scores = jnp.where(live, scores, MASKED)
            row_max = jnp.max(scores, axis=1, keepdims=True)
            e = jnp.where(live, jnp.exp(scores - row_max), 0.0)
            row_total = jnp.sum(e, axis=1, keepdims=True)
            part_out = lax.dot_general(
                e.astype(jnp.bfloat16), keys[:latent],
                (((1,), (1,)), ((), ())), preferred_element_type=jnp.float32,
            )
            for t in range(n_tp):
                mine = slice(t * share, (t + 1) * share)
                for c in range(chunks):
                    res_out[t, r, c * share : (c + 1) * share] = part_out[
                        mine, c * 128 : (c + 1) * 128
                    ]
                res_out[t, r, chunks * share :, :share] = stats_rows(
                    row_max[mine], row_total[mine], 0.0, 0.0
                )
        if n_tp > 1:
            pl.semaphore_wait(barrier, n_tp - 1)
        for k in range(1, n_tp):
            res_copy(lax.rem(tp + k, n_tp), tp).start()
        res_in[tp] = res_out[tp]
        for k in range(1, n_tp):
            peer = lax.rem(tp + k, n_tp)
            res_copy(peer, peer).wait_recv()

        def columns(block):
            wide = jnp.concatenate([block[:, :share], jnp.zeros((8, 128 - share))], axis=1)
            turned = wide.T
            return [turned[:share, i : i + 1] for i in range(4)]

        def joined(block, scale, sums):
            return [
                sums[c] + block[c * share : (c + 1) * share] * scale for c in range(chunks)
            ]

        tail = slice(chunks * share, chunks * share + 8)
        resident = []
        for r in range(rows):
            parts = [columns(res_in[t, r, tail]) for t in range(n_tp)]
            joint = functools.reduce(jnp.maximum, [part[0] for part in parts])
            total = jnp.zeros((share, 1), jnp.float32)
            sums = [jnp.zeros((share, 128), jnp.float32)] * chunks
            for t in range(n_tp):
                scale = jnp.exp(parts[t][0] - joint)
                total += parts[t][1] * scale
                sums = joined(res_in[t, r], scale, sums)
            for c in range(chunks):
                res_sum[r, c * share : (c + 1) * share] = sums[c]
            resident.append((joint, total))
        for p in range(n_seq * n_tp):
            stat_copy(0, 0, p).wait_recv()
        pieces = [columns(stat_in[p]) for p in range(n_seq * n_tp)]
        for r in range(rows):
            row_max, row_total = resident[r]
            maxima = [
                jnp.where(slot == float(r), piece_max, MASKED) for piece_max, _, slot, _ in pieces
            ]
            joint = functools.reduce(jnp.maximum, maxima, row_max)
            factor = jnp.exp(row_max - joint)
            factors = [
                jnp.where(pieces[p][2] == float(r), jnp.exp(maxima[p] - joint), 0.0)
                for p in range(n_seq * n_tp)
            ]
            total = row_total * factor
            for p in range(n_seq * n_tp):
                total += pieces[p][1] * factors[p]
            inverse = 1.0 / total
            for p in range(n_seq * n_tp):
                scales[r, p] = jnp.broadcast_to(factors[p] * pieces[p][3] * inverse, (share, 128))
            for c in range(chunks):
                block = slice(c * share, (c + 1) * share)
                res_sum[r, block] = res_sum[r, block] * (factor * inverse)
        for p in range(n_seq * n_tp):
            piece_copy(0, 0, p).wait_recv()
        for c in range(chunks):
            block = slice(c * share, (c + 1) * share)
            sums = [res_sum[r, block] for r in range(rows)]
            for p in range(n_seq * n_tp):
                value = piece_in[p][block].astype(jnp.int32).astype(jnp.float32)
                sums = [sums[r] + value * scales[r, p] for r in range(rows)]
            for r in range(rows):
                out_ref[0, r, :, c * 128 : (c + 1) * 128] = sums[r].astype(out_ref.dtype)
        for k in range(1, n_tp):
            res_copy(lax.rem(tp + k, n_tp), tp).wait_send()


def local(
    n_seq, n_tp,
    page_pool, queries, block_table, res_len, piece_len, piece_owner, piece_slot, piece_pos, kv_gain
):
    pages, page, width = page_pool.shape
    rows, heads, _ = queries.shape
    latent = kv_gain.shape[0]
    share = heads // n_tp
    packed = latent // 128 * share + 8
    vmem = pl.BlockSpec(memory_space=pltpu.VMEM)
    parts = n_seq * n_tp
    return pl.pallas_call(
        functools.partial(kernel, n_seq, n_tp),
        out_shape=jax.ShapeDtypeStruct((1, rows, share, latent), jnp.bfloat16),
        in_specs=[pl.BlockSpec(memory_space=pltpu.HBM)] * 9,
        out_specs=vmem,
        scratch_shapes=[
            pltpu.VMEM(queries.shape, jnp.bfloat16),
            pltpu.SMEM(block_table.shape, jnp.int32),
            pltpu.SMEM(res_len.shape[::-1], jnp.int32),
            pltpu.SMEM(piece_len.shape, jnp.int32),
            pltpu.SMEM(piece_len.shape, jnp.int32),
            pltpu.SMEM(piece_len.shape, jnp.int32),
            pltpu.SMEM(piece_len.shape, jnp.int32),
            pltpu.VMEM((1, latent), jnp.float32),
            pltpu.SemaphoreType.DMA((8,)),
            pltpu.VMEM((pages, width, page), jnp.bfloat16),
            pltpu.VMEM((width, FRESH_DEV), jnp.bfloat16),
            pltpu.VMEM((n_seq, heads, width), jnp.bfloat16),
            pltpu.VMEM((n_seq, heads, width), jnp.bfloat16),
            pltpu.VMEM((n_seq, 8, 128), jnp.int32),
            pltpu.VMEM((n_seq, 8, 128), jnp.int32),
            pltpu.VMEM((n_seq, n_tp, packed - 8, 128), jnp.int16),
            pltpu.VMEM((parts, packed - 8, 128), jnp.int16),
            pltpu.VMEM((n_seq, n_tp, 8, 128), jnp.float32),
            pltpu.VMEM((parts, 8, 128), jnp.float32),
            pltpu.VMEM((rows, parts, share, 128), jnp.float32),
            pltpu.VMEM((n_tp, rows, packed, 128), jnp.float32),
            pltpu.VMEM((n_tp, rows, packed, 128), jnp.float32),
            pltpu.VMEM((rows, packed, 128), jnp.float32),
            pltpu.SemaphoreType.DMA,
            pltpu.SemaphoreType.DMA((n_seq,)),
            pltpu.SemaphoreType.DMA((n_seq,)),
            pltpu.SemaphoreType.DMA((n_seq,)),
            pltpu.SemaphoreType.DMA((n_seq,)),
            pltpu.SemaphoreType.DMA((parts,)),
            pltpu.SemaphoreType.DMA((parts,)),
            pltpu.SemaphoreType.DMA((parts,)),
            pltpu.SemaphoreType.DMA((parts,)),
            pltpu.SemaphoreType.DMA((n_tp,)),
            pltpu.SemaphoreType.DMA((n_tp,)),
        ],
        compiler_params=pltpu.CompilerParams(
            collective_id=0, has_side_effects=True, vmem_limit_bytes=32 * 1024 * 1024
        ),
    )(
        *[
            pltpu.with_memory_space_constraint(operand, pltpu.HBM)
            for operand in (
                jnp.swapaxes(page_pool, 1, 2), queries, block_table, res_len.T, piece_len,
                piece_owner, piece_slot, piece_pos, kv_gain[None],
            )
        ]
    )


def solution(mesh):
    return jax.shard_map(
        functools.partial(local, mesh.shape["seq"], mesh.shape["tp"]),
        mesh=mesh,
        in_specs=(
            P(("groups", "seq", "tp", "section"), None, None),
            P(("groups", "seq"), None, None),
            P(("groups", "seq"), "tp", None),
            P(("groups", "seq"), "tp"),
            P(("groups", "seq"), "tp", None),
            P(("groups", "seq"), "tp", None),
            P(("groups", "seq"), "tp", None),
            P(("groups", "seq"), "tp", None),
            P(),
        ),
        out_specs=P("section", ("groups", "seq"), "tp", None),
        check_vma=False,
    )
```

```python
import functools

import jax
import jax.numpy as jnp
import numpy as np
from jax import lax
from jax.experimental import pallas as pl
from jax.experimental.pallas import tpu as pltpu
from jax.sharding import PartitionSpec as P

FRESH_DEV = 1024
SOFT_SCALE = 192.0 ** (-0.5)
MASKED = -1e30
NORM_EPSILON = 1e-06
GROUP = 2
STEPS = 32700.0
MESH = pl.DeviceIdType.MESH


def stats_rows(row_max, row_total, slot, step):
    lane = lax.broadcasted_iota(jnp.int32, (row_max.shape[0], 128), 1)
    block = jnp.where(
        lane == 0, row_max, jnp.where(lane == 1, row_total, jnp.where(lane == 2, slot, step))
    )
    return block.T[:8]


def cos_sin(angles):
    turns = jnp.floor(angles * (2.0 / np.pi) + 0.5)
    rest = angles - turns * 1.5703125
    rest = rest - turns * 4.837512969970703125e-4
    rest = rest - turns * 7.54978995489188216e-8
    square = rest * rest
    sine = rest + rest * square * (
        -1.6666654611e-1 + square * (8.3321608736e-3 + square * -1.9515295891e-4)
    )
    cosine = (
        1.0
        - 0.5 * square
        + square * square
        * (4.166664568298827e-2 + square * (-1.388731625493765e-3 + square * 2.443315711809948e-5))
    )
    quarter = turns.astype(jnp.int32) & 3
    odd = (quarter & 1) == 1
    cos_value = jnp.where(odd, sine, cosine)
    sin_value = jnp.where(odd, cosine, sine)
    cos_value = jnp.where((quarter == 1) | (quarter == 2), -cos_value, cos_value)
    sin_value = jnp.where(quarter >= 2, -sin_value, sin_value)
    return cos_value, sin_value


def kernel(
    n_seq, n_tp, pool_hbm, q_hbm, table_hbm, res_hbm, len_hbm, owner_hbm, slot_hbm, pos_hbm,
    gain_hbm, out_ref,
    q_ref, table_ref, res_ref, len_ref, owner_ref, slot_ref, pos_ref, gain_ref, load_sem,
    pool, fresh, q_in, q_out, meta_in, meta_out, piece_out, piece_in, stat_out, stat_in, scales, res_out, res_in, res_sum,
    pool_sem, meta_send, meta_recv, q_send, q_recv, piece_send, piece_recv, stat_send, stat_recv,
    res_send, res_recv,
):
    pages, width, page = pool.shape
    rows, heads, _ = q_ref.shape
    latent = gain_ref.shape[1]
    half = (width - latent) // 2
    share = heads // n_tp
    fresh_pages = FRESH_DEV // page
    chunks = latent // 128
    seq = lax.axis_index("seq")
    tp = lax.axis_index("tp")
    section = lax.axis_index("section")
    barrier = pltpu.get_barrier_semaphore()
    order = [lax.rem((seq // 2) * 2 + i, n_seq) for i in range(n_seq)]
    peers = [(seq // 2) * 2 + 1 - lax.rem(seq, 2)] + order[2:]

    loads = [
        pltpu.make_async_copy(source, target, load_sem.at[i])
        for i, (source, target) in enumerate(
            [
                (len_hbm, len_ref), (owner_hbm, owner_ref), (slot_hbm, slot_ref),
                (pos_hbm, pos_ref), (table_hbm, table_ref), (res_hbm, res_ref),
                (q_hbm, q_ref), (gain_hbm, gain_ref),
            ]
        )
    ]
    def at(s, t, c):
        return {"seq": s, "tp": t, "section": c}

    def meta_copy(peer, own):
        return pltpu.make_async_remote_copy(
            meta_out.at[peer], meta_in.at[own], meta_send.at[peer], meta_recv.at[own],
            device_id=at(peer, tp, 0), device_id_type=MESH,
        )

    def q_copy(peer, own):
        return pltpu.make_async_remote_copy(
            q_out.at[peer], q_in.at[own], q_send.at[peer], q_recv.at[own],
            device_id=at(peer, tp, 0), device_id_type=MESH,
        )

    def piece_copy(i, t, own):
        return pltpu.make_async_remote_copy(
            piece_out.at[i, t], piece_in.at[own], piece_send.at[i * n_tp + t], piece_recv.at[own],
            device_id=at(order[i], t, 1), device_id_type=MESH,
        )

    def stat_copy(i, t, own):
        return pltpu.make_async_remote_copy(
            stat_out.at[i, t], stat_in.at[own], stat_send.at[i * n_tp + t], stat_recv.at[own],
            device_id=at(order[i], t, 1), device_id_type=MESH,
        )

    def res_copy(t, own):
        return pltpu.make_async_remote_copy(
            res_out.at[t], res_in.at[own], res_send.at[t], res_recv.at[own],
            device_id=at(seq, t, 1), device_id_type=MESH,
        )

    @pl.when(section == 0)
    def prefill():
        raw_copy = pltpu.make_async_copy(
            pool_hbm.at[pl.ds(0, fresh_pages)], pool.at[pl.ds(0, fresh_pages)], pool_sem
        )
        for peer in peers:
            pl.semaphore_signal(barrier, inc=1, device_id=at(peer, tp, 0), device_id_type=MESH)
        for load in loads:
            load.start()
        raw_copy.start()
        for load in loads:
            load.wait()

        lengths = [len_ref[0, 0, k] for k in range(n_seq)]
        begins = [jnp.int32(0)]
        for k in range(n_seq - 1):
            begins.append(begins[-1] + lengths[k])

        def of_owner(d, values):
            total = jnp.int32(0)
            for k in range(n_seq):
                total = total + jnp.where(owner_ref[0, 0, k] == d, values[k], 0)
            return total

        slots = [slot_ref[0, 0, k] for k in range(n_seq)]
        owner_begin = [of_owner(d, begins) for d in order]
        owner_len = [of_owner(d, lengths) for d in order]
        owner_slot = [of_owner(d, slots) for d in order]
        for i, d in enumerate(order):
            meta_out[d] = jnp.full(meta_out.shape[1:], owner_slot[i], jnp.int32)

        pl.semaphore_wait(barrier, n_seq - 1 + n_seq * n_tp)
        for peer in peers:
            meta_copy(peer, seq).start()

        for peer in peers:
            meta_copy(peer, peer).wait_recv()
            wanted = meta_in[peer][0:1, 0:1]
            picked = q_ref[0].astype(jnp.float32)
            for r in range(1, rows):
                picked = jnp.where(wanted == r, q_ref[r].astype(jnp.float32), picked)
            q_out[peer] = picked.astype(jnp.bfloat16)
            q_copy(peer, seq).start()
        own_slot = meta_out[seq][0:1, 0:1]
        picked = q_ref[0].astype(jnp.float32)
        for r in range(1, rows):
            picked = jnp.where(own_slot == r, q_ref[r].astype(jnp.float32), picked)
        q_in[seq] = picked.astype(jnp.bfloat16)

        out_ref[...] = jnp.zeros_like(out_ref)
        raw_copy.wait()
        gain = jnp.broadcast_to(gain_ref[...], (page, latent)).T
        index = lax.broadcasted_iota(jnp.int32, (half, page), 0)
        freq = jnp.ones((half, page), jnp.float32)
        for i in range(1, half):
            freq = jnp.where(index == i, float(10000.0 ** (-i / half)), freq)
        for j in range(fresh_pages):
            x = pool[j, :latent].astype(jnp.float32)
            mean = jnp.mean(x * x, axis=0, keepdims=True)
            columns = slice(j * page, (j + 1) * page)
            normed = x * lax.rsqrt(mean + NORM_EPSILON) * gain
            fresh[:latent, columns] = normed.astype(jnp.bfloat16)
            y = pool[j, latent:].astype(jnp.float32)
            a, b = y[:half], y[half:]
            token = lax.broadcasted_iota(jnp.int32, (1, page), 1) + j * page
            shift = jnp.zeros((1, page), jnp.int32)
            for k in range(n_seq):
                live = (token >= begins[k]) & (token < begins[k] + lengths[k])
                shift = jnp.where(live, pos_ref[0, 0, k] - begins[k], shift)
            cosine, sine = cos_sin((token + shift).astype(jnp.float32) * freq)
            turned = jnp.concatenate([a * cosine - b * sine, b * cosine + a * sine], axis=0)
            fresh[latent:, columns] = turned.astype(jnp.bfloat16)

        out_ref[...] = jnp.zeros_like(out_ref)
        tokens = lax.broadcasted_iota(jnp.int32, (1, FRESH_DEV), 1)
        for first in range(0, n_seq, GROUP):
            for d in peers[max(first - 1, 0) : first + GROUP - 1]:
                q_copy(d, d).wait_recv()
            members = range(first, first + GROUP)
            wide = jnp.concatenate([q_in[order[i]] for i in members], axis=0)
            scores = jnp.dot(wide, fresh[...], preferred_element_type=jnp.float32) * SOFT_SCALE
            stats = []
            weights = []
            for i in members:
                live = (tokens >= owner_begin[i]) & (tokens < owner_begin[i] + owner_len[i])
                here = (i - first) * heads
                part = jnp.where(live, scores[here : here + heads], MASKED)
                row_max = jnp.max(part, axis=1, keepdims=True)
                e = jnp.where(live, jnp.exp(part - row_max), 0.0)
                row_total = jnp.sum(e, axis=1, keepdims=True)
                weights.append(e.astype(jnp.bfloat16))
                stats.append((row_max, row_total, owner_slot[i].astype(jnp.float32)))
            group_out = lax.dot_general(
                jnp.concatenate(weights, axis=0), fresh[:latent],
                (((1,), (1,)), ((), ())), preferred_element_type=jnp.float32,
            )
            step = jnp.maximum(jnp.max(jnp.abs(group_out), axis=1, keepdims=True), 1e-30) / STEPS
            turned = stats_rows(
                jnp.concatenate([stats[i - first][0] for i in members], axis=0),
                jnp.concatenate([stats[i - first][1] for i in members], axis=0),
                jnp.concatenate(
                    [jnp.full((heads, 1), stats[i - first][2], jnp.float32) for i in members],
                    axis=0,
                ),
                step,
            )
            for i in members:
                for t in range(n_tp):
                    here = (i - first) * heads + t * share
                    stat_out[i, t, :, :share] = turned[:, here : here + share]
                    stat_copy(i, t, seq * n_tp + tp).start()
            counted = jnp.floor(group_out * (1.0 / step) + 0.5)
            for i in members:
                for t in range(n_tp):
                    here = (i - first) * heads + t * share
                    stacked = jnp.concatenate(
                        [
                            counted[here : here + share, c * 128 : (c + 1) * 128]
                            for c in range(chunks)
                        ],
                        axis=0,
                    )
                    piece_out[i, t] = stacked.astype(jnp.int32).astype(jnp.int16)
                    piece_copy(i, t, seq * n_tp + tp).start()

        for peer in peers:
            meta_copy(peer, peer).wait_send()
            q_copy(peer, peer).wait_send()
        for d in range(n_seq):
            for t in range(n_tp):
                piece_copy(d, t, 0).wait_send()
                stat_copy(d, t, 0).wait_send()

    @pl.when(section == 1)
    def decode():
        pool_copy = pltpu.make_async_copy(pool_hbm, pool, pool_sem)
        for s in range(n_seq):
            for t in range(n_tp):
                pl.semaphore_signal(barrier, inc=1, device_id=at(s, t, 0), device_id_type=MESH)
        for k in range(1, n_tp):
            pl.semaphore_signal(
                barrier, inc=1, device_id=at(seq, lax.rem(tp + k, n_tp), 1), device_id_type=MESH
            )
        for load in loads:
            load.start()
        pool_copy.start()
        for load in loads:
            load.wait()
        pool_copy.wait()
        most = table_ref.shape[2]
        tokens = lax.broadcasted_iota(jnp.int32, (1, most * page), 1)
        for r in range(rows):
            keys = jnp.concatenate([pool[table_ref[r, 0, j]] for j in range(most)], axis=1)
            scores = jnp.dot(q_ref[r], keys, preferred_element_type=jnp.float32) * SOFT_SCALE
            live = tokens < res_ref[0, r]
            scores = jnp.where(live, scores, MASKED)
            row_max = jnp.max(scores, axis=1, keepdims=True)
            e = jnp.where(live, jnp.exp(scores - row_max), 0.0)
            row_total = jnp.sum(e, axis=1, keepdims=True)
            part_out = lax.dot_general(
                e.astype(jnp.bfloat16), keys[:latent],
                (((1,), (1,)), ((), ())), preferred_element_type=jnp.float32,
            )
            for t in range(n_tp):
                mine = slice(t * share, (t + 1) * share)
                for c in range(chunks):
                    res_out[t, r, c * share : (c + 1) * share] = part_out[
                        mine, c * 128 : (c + 1) * 128
                    ]
                res_out[t, r, chunks * share :, :share] = stats_rows(
                    row_max[mine], row_total[mine], 0.0, 0.0
                )
        if n_tp > 1:
            pl.semaphore_wait(barrier, n_tp - 1)
        for k in range(1, n_tp):
            res_copy(lax.rem(tp + k, n_tp), tp).start()
        res_in[tp] = res_out[tp]
        for k in range(1, n_tp):
            peer = lax.rem(tp + k, n_tp)
            res_copy(peer, peer).wait_recv()

        def columns(block):
            wide = jnp.concatenate([block[:, :share], jnp.zeros((8, 128 - share))], axis=1)
            turned = wide.T
            return [turned[:share, i : i + 1] for i in range(4)]

        def joined(block, scale, sums):
            return [
                sums[c] + block[c * share : (c + 1) * share] * scale for c in range(chunks)
            ]

        tail = slice(chunks * share, chunks * share + 8)
        resident = []
        for r in range(rows):
            parts = [columns(res_in[t, r, tail]) for t in range(n_tp)]
            joint = functools.reduce(jnp.maximum, [part[0] for part in parts])
            total = jnp.zeros((share, 1), jnp.float32)
            sums = [jnp.zeros((share, 128), jnp.float32)] * chunks
            for t in range(n_tp):
                scale = jnp.exp(parts[t][0] - joint)
                total += parts[t][1] * scale
                sums = joined(res_in[t, r], scale, sums)
            for c in range(chunks):
                res_sum[r, c * share : (c + 1) * share] = sums[c]
            lines = [res_in[t, r, tail] for t in range(n_tp)]
            joint = functools.reduce(jnp.maximum, [line[0:1] for line in lines])
            total = sum(line[1:2] * jnp.exp(line[0:1] - joint) for line in lines)
            resident.append((joint, total))
        for p in range(n_seq * n_tp):
            stat_copy(0, 0, p).wait_recv()
        count = n_seq * n_tp
        piece_max, piece_total, piece_slot, piece_step = [stat_in[:, i, :] for i in range(4)]
        mixed, kept = [], []
        for r in range(rows):
            row_max, row_total = resident[r]
            member = piece_slot == float(r)
            maxima = jnp.where(member, piece_max, MASKED)
            joint = jnp.maximum(jnp.max(maxima, axis=0, keepdims=True), row_max)
            factor = jnp.exp(row_max - joint)
            factors = jnp.where(member, jnp.exp(maxima - joint), 0.0)
            total = row_total * factor + jnp.sum(piece_total * factors, axis=0, keepdims=True)
            inverse = 1.0 / total
            mixed.append(factors * piece_step * inverse)
            kept.append(factor * inverse)
        used = rows * count + rows
        mixed += kept + [jnp.zeros((-used % 128, 128), jnp.float32)]
        turned = jnp.concatenate(mixed, axis=0).T
        for r in range(rows):
            for p in range(count):
                at_p = r * count + p
                scales[r, p] = jnp.broadcast_to(turned[:share, at_p : at_p + 1], (share, 128))
            at_r = rows * count + r
            factor = turned[:share, at_r : at_r + 1]
            for c in range(chunks):
                block = slice(c * share, (c + 1) * share)
                res_sum[r, block] = res_sum[r, block] * factor
        for p in range(n_seq * n_tp):
            piece_copy(0, 0, p).wait_recv()
        for c in range(chunks):
            block = slice(c * share, (c + 1) * share)
            sums = [res_sum[r, block] for r in range(rows)]
            for p in range(n_seq * n_tp):
                value = piece_in[p][block].astype(jnp.int32).astype(jnp.float32)
                sums = [sums[r] + value * scales[r, p] for r in range(rows)]
            for r in range(rows):
                out_ref[0, r, :, c * 128 : (c + 1) * 128] = sums[r].astype(out_ref.dtype)
        for k in range(1, n_tp):
            res_copy(lax.rem(tp + k, n_tp), tp).wait_send()


def local(
    n_seq, n_tp,
    page_pool, queries, block_table, res_len, piece_len, piece_owner, piece_slot, piece_pos, kv_gain
):
    pages, page, width = page_pool.shape
    rows, heads, _ = queries.shape
    latent = kv_gain.shape[0]
    share = heads // n_tp
    packed = latent // 128 * share + 8
    vmem = pl.BlockSpec(memory_space=pltpu.VMEM)
    parts = n_seq * n_tp
    return pl.pallas_call(
        functools.partial(kernel, n_seq, n_tp),
        out_shape=jax.ShapeDtypeStruct((1, rows, share, latent), jnp.bfloat16),
        in_specs=[pl.BlockSpec(memory_space=pltpu.HBM)] * 9,
        out_specs=vmem,
        scratch_shapes=[
            pltpu.VMEM(queries.shape, jnp.bfloat16),
            pltpu.SMEM(block_table.shape, jnp.int32),
            pltpu.SMEM(res_len.shape[::-1], jnp.int32),
            pltpu.SMEM(piece_len.shape, jnp.int32),
            pltpu.SMEM(piece_len.shape, jnp.int32),
            pltpu.SMEM(piece_len.shape, jnp.int32),
            pltpu.SMEM(piece_len.shape, jnp.int32),
            pltpu.VMEM((1, latent), jnp.float32),
            pltpu.SemaphoreType.DMA((8,)),
            pltpu.VMEM((pages, width, page), jnp.bfloat16),
            pltpu.VMEM((width, FRESH_DEV), jnp.bfloat16),
            pltpu.VMEM((n_seq, heads, width), jnp.bfloat16),
            pltpu.VMEM((n_seq, heads, width), jnp.bfloat16),
            pltpu.VMEM((n_seq, 8, 128), jnp.int32),
            pltpu.VMEM((n_seq, 8, 128), jnp.int32),
            pltpu.VMEM((n_seq, n_tp, packed - 8, 128), jnp.int16),
            pltpu.VMEM((parts, packed - 8, 128), jnp.int16),
            pltpu.VMEM((n_seq, n_tp, 8, 128), jnp.float32),
            pltpu.VMEM((parts, 8, 128), jnp.float32),
            pltpu.VMEM((rows, parts, share, 128), jnp.float32),
            pltpu.VMEM((n_tp, rows, packed, 128), jnp.float32),
            pltpu.VMEM((n_tp, rows, packed, 128), jnp.float32),
            pltpu.VMEM((rows, packed, 128), jnp.float32),
            pltpu.SemaphoreType.DMA,
            pltpu.SemaphoreType.DMA((n_seq,)),
            pltpu.SemaphoreType.DMA((n_seq,)),
            pltpu.SemaphoreType.DMA((n_seq,)),
            pltpu.SemaphoreType.DMA((n_seq,)),
            pltpu.SemaphoreType.DMA((parts,)),
            pltpu.SemaphoreType.DMA((parts,)),
            pltpu.SemaphoreType.DMA((parts,)),
            pltpu.SemaphoreType.DMA((parts,)),
            pltpu.SemaphoreType.DMA((n_tp,)),
            pltpu.SemaphoreType.DMA((n_tp,)),
        ],
        compiler_params=pltpu.CompilerParams(
            collective_id=0, has_side_effects=True, vmem_limit_bytes=32 * 1024 * 1024
        ),
    )(
        *[
            pltpu.with_memory_space_constraint(operand, pltpu.HBM)
            for operand in (
                jnp.swapaxes(page_pool, 1, 2), queries, block_table, res_len.T, piece_len,
                piece_owner, piece_slot, piece_pos, kv_gain[None],
            )
        ]
    )


def solution(mesh):
    return jax.shard_map(
        functools.partial(local, mesh.shape["seq"], mesh.shape["tp"]),
        mesh=mesh,
        in_specs=(
            P(("groups", "seq", "tp", "section"), None, None),
            P(("groups", "seq"), None, None),
            P(("groups", "seq"), "tp", None),
            P(("groups", "seq"), "tp"),
            P(("groups", "seq"), "tp", None),
            P(("groups", "seq"), "tp", None),
            P(("groups", "seq"), "tp", None),
            P(("groups", "seq"), "tp", None),
            P(),
        ),
        out_specs=P("section", ("groups", "seq"), "tp", None),
        check_vma=False,
    )
```

```python
import functools

import jax
import jax.numpy as jnp
import numpy as np
from jax import lax
from jax.experimental import pallas as pl
from jax.experimental.pallas import tpu as pltpu
from jax.sharding import PartitionSpec as P

FRESH_DEV = 1024
SOFT_SCALE = 192.0 ** (-0.5)
MASKED = -1e30
NORM_EPSILON = 1e-06
GROUP = 2
STEPS = 32700.0
MESH = pl.DeviceIdType.MESH


def stats_rows(row_max, row_total, slot, step):
    lane = lax.broadcasted_iota(jnp.int32, (row_max.shape[0], 128), 1)
    block = jnp.where(
        lane == 0, row_max, jnp.where(lane == 1, row_total, jnp.where(lane == 2, slot, step))
    )
    return block.T[:8]


def cos_sin(angles):
    turns = jnp.floor(angles * (2.0 / np.pi) + 0.5)
    rest = angles - turns * 1.5703125
    rest = rest - turns * 4.837512969970703125e-4
    rest = rest - turns * 7.54978995489188216e-8
    square = rest * rest
    sine = rest + rest * square * (
        -1.6666654611e-1 + square * (8.3321608736e-3 + square * -1.9515295891e-4)
    )
    cosine = (
        1.0
        - 0.5 * square
        + square * square
        * (4.166664568298827e-2 + square * (-1.388731625493765e-3 + square * 2.443315711809948e-5))
    )
    quarter = turns.astype(jnp.int32) & 3
    odd = (quarter & 1) == 1
    cos_value = jnp.where(odd, sine, cosine)
    sin_value = jnp.where(odd, cosine, sine)
    cos_value = jnp.where((quarter == 1) | (quarter == 2), -cos_value, cos_value)
    sin_value = jnp.where(quarter >= 2, -sin_value, sin_value)
    return cos_value, sin_value


def kernel(
    n_seq, n_tp, pool_hbm, q_hbm, table_hbm, res_hbm, len_hbm, owner_hbm, slot_hbm, pos_hbm,
    gain_hbm, out_ref,
    q_ref, table_ref, res_ref, len_ref, owner_ref, slot_ref, pos_ref, gain_ref, load_sem,
    pool, fresh, q_in, q_out, meta_in, meta_out, piece_out, piece_in, stat_out, stat_in, scales, res_out, res_in, res_sum,
    pool_sem, meta_send, meta_recv, q_send, q_recv, piece_send, piece_recv, stat_send, stat_recv,
    res_send, res_recv,
):
    pages, width, page = pool.shape
    rows, heads, _ = q_ref.shape
    latent = gain_ref.shape[1]
    half = (width - latent) // 2
    share = heads // n_tp
    fresh_pages = FRESH_DEV // page
    chunks = latent // 128
    seq = lax.axis_index("seq")
    tp = lax.axis_index("tp")
    section = lax.axis_index("section")
    barrier = pltpu.get_barrier_semaphore()
    order = [lax.rem((seq // 2) * 2 + i, n_seq) for i in range(n_seq)]
    peers = [(seq // 2) * 2 + 1 - lax.rem(seq, 2)] + order[2:]

    loads = [
        pltpu.make_async_copy(source, target, load_sem.at[i])
        for i, (source, target) in enumerate(
            [
                (len_hbm, len_ref), (owner_hbm, owner_ref), (slot_hbm, slot_ref),
                (pos_hbm, pos_ref), (table_hbm, table_ref), (res_hbm, res_ref),
                (q_hbm, q_ref), (gain_hbm, gain_ref),
            ]
        )
    ]
    def at(s, t, c):
        return {"seq": s, "tp": t, "section": c}

    def meta_copy(peer, own):
        return pltpu.make_async_remote_copy(
            meta_out.at[peer], meta_in.at[own], meta_send.at[peer], meta_recv.at[own],
            device_id=at(peer, tp, 0), device_id_type=MESH,
        )

    def q_copy(peer, own):
        return pltpu.make_async_remote_copy(
            q_out.at[peer], q_in.at[own], q_send.at[peer], q_recv.at[own],
            device_id=at(peer, tp, 0), device_id_type=MESH,
        )

    def piece_copy(i, t, own):
        return pltpu.make_async_remote_copy(
            piece_out.at[i, t], piece_in.at[own], piece_send.at[i * n_tp + t], piece_recv.at[own],
            device_id=at(order[i], t, 1), device_id_type=MESH,
        )

    def stat_copy(i, t, own):
        return pltpu.make_async_remote_copy(
            stat_out.at[i, t], stat_in.at[own], stat_send.at[i * n_tp + t], stat_recv.at[own],
            device_id=at(order[i], t, 1), device_id_type=MESH,
        )

    def res_copy(t, own):
        return pltpu.make_async_remote_copy(
            res_out.at[t], res_in.at[own], res_send.at[t], res_recv.at[own],
            device_id=at(seq, t, 1), device_id_type=MESH,
        )

    @pl.when(section == 0)
    def prefill():
        raw_copy = pltpu.make_async_copy(
            pool_hbm.at[pl.ds(0, fresh_pages)], pool.at[pl.ds(0, fresh_pages)], pool_sem
        )
        for peer in peers:
            pl.semaphore_signal(barrier, inc=1, device_id=at(peer, tp, 0), device_id_type=MESH)
        for load in loads:
            load.start()
        raw_copy.start()
        for load in loads:
            load.wait()

        lengths = [len_ref[0, 0, k] for k in range(n_seq)]
        begins = [jnp.int32(0)]
        for k in range(n_seq - 1):
            begins.append(begins[-1] + lengths[k])

        def of_owner(d, values):
            total = jnp.int32(0)
            for k in range(n_seq):
                total = total + jnp.where(owner_ref[0, 0, k] == d, values[k], 0)
            return total

        slots = [slot_ref[0, 0, k] for k in range(n_seq)]
        owner_begin = [of_owner(d, begins) for d in order]
        owner_len = [of_owner(d, lengths) for d in order]
        owner_slot = [of_owner(d, slots) for d in order]
        for i, d in enumerate(order):
            meta_out[d] = jnp.full(meta_out.shape[1:], owner_slot[i], jnp.int32)

        pl.semaphore_wait(barrier, n_seq - 1 + n_seq * n_tp)
        for peer in peers:
            meta_copy(peer, seq).start()

        for peer in peers:
            meta_copy(peer, peer).wait_recv()
            wanted = meta_in[peer][0:1, 0:1]
            picked = q_ref[0].astype(jnp.float32)
            for r in range(1, rows):
                picked = jnp.where(wanted == r, q_ref[r].astype(jnp.float32), picked)
            q_out[peer] = picked.astype(jnp.bfloat16)
            q_copy(peer, seq).start()
        own_slot = meta_out[seq][0:1, 0:1]
        picked = q_ref[0].astype(jnp.float32)
        for r in range(1, rows):
            picked = jnp.where(own_slot == r, q_ref[r].astype(jnp.float32), picked)
        q_in[seq] = picked.astype(jnp.bfloat16)

        out_ref[...] = jnp.zeros_like(out_ref)
        raw_copy.wait()
        gain = jnp.broadcast_to(gain_ref[...], (page, latent)).T
        index = lax.broadcasted_iota(jnp.int32, (half, page), 0)
        freq = jnp.ones((half, page), jnp.float32)
        for i in range(1, half):
            freq = jnp.where(index == i, float(10000.0 ** (-i / half)), freq)
        for j in range(fresh_pages):
            x = pool[j, :latent].astype(jnp.float32)
            mean = jnp.mean(x * x, axis=0, keepdims=True)
            columns = slice(j * page, (j + 1) * page)
            normed = x * lax.rsqrt(mean + NORM_EPSILON) * gain
            fresh[:latent, columns] = normed.astype(jnp.bfloat16)
            y = pool[j, latent:].astype(jnp.float32)
            a, b = y[:half], y[half:]
            token = lax.broadcasted_iota(jnp.int32, (1, page), 1) + j * page
            shift = jnp.zeros((1, page), jnp.int32)
            for k in range(n_seq):
                live = (token >= begins[k]) & (token < begins[k] + lengths[k])
                shift = jnp.where(live, pos_ref[0, 0, k] - begins[k], shift)
            cosine, sine = cos_sin((token + shift).astype(jnp.float32) * freq)
            turned = jnp.concatenate([a * cosine - b * sine, b * cosine + a * sine], axis=0)
            fresh[latent:, columns] = turned.astype(jnp.bfloat16)

        out_ref[...] = jnp.zeros_like(out_ref)
        tokens = lax.broadcasted_iota(jnp.int32, (1, FRESH_DEV), 1)
        for first in range(0, n_seq, GROUP):
            for d in peers[max(first - 1, 0) : first + GROUP - 1]:
                q_copy(d, d).wait_recv()
            members = range(first, first + GROUP)
            wide = jnp.concatenate([q_in[order[i]] for i in members], axis=0)
            scores = jnp.dot(wide, fresh[...], preferred_element_type=jnp.float32) * SOFT_SCALE
            stats = []
            weights = []
            for i in members:
                live = (tokens >= owner_begin[i]) & (tokens < owner_begin[i] + owner_len[i])
                here = (i - first) * heads
                part = jnp.where(live, scores[here : here + heads], MASKED)
                row_max = jnp.max(part, axis=1, keepdims=True)
                e = jnp.where(live, jnp.exp(part - row_max), 0.0)
                row_total = jnp.sum(e, axis=1, keepdims=True)
                weights.append(e.astype(jnp.bfloat16))
                stats.append((row_max, row_total, owner_slot[i].astype(jnp.float32)))
            group_out = lax.dot_general(
                jnp.concatenate(weights, axis=0), fresh[:latent],
                (((1,), (1,)), ((), ())), preferred_element_type=jnp.float32,
            )
            step = jnp.maximum(jnp.max(jnp.abs(group_out), axis=1, keepdims=True), 1e-30) / STEPS
            turned = stats_rows(
                jnp.concatenate([stats[i - first][0] for i in members], axis=0),
                jnp.concatenate([stats[i - first][1] for i in members], axis=0),
                jnp.concatenate(
                    [jnp.full((heads, 1), stats[i - first][2], jnp.float32) for i in members],
                    axis=0,
                ),
                step,
            )
            for i in members:
                for t in range(n_tp):
                    here = (i - first) * heads + t * share
                    stat_out[i, t, :, :share] = turned[:, here : here + share]
                    stat_copy(i, t, seq * n_tp + tp).start()
            counted = jnp.floor(group_out * (1.0 / step) + 0.5)
            for i in members:
                for t in range(n_tp):
                    here = (i - first) * heads + t * share
                    stacked = jnp.concatenate(
                        [
                            counted[here : here + share, c * 128 : (c + 1) * 128]
                            for c in range(chunks)
                        ],
                        axis=0,
                    )
                    piece_out[i, t] = stacked.astype(jnp.int32).astype(jnp.int16)
                    piece_copy(i, t, seq * n_tp + tp).start()

        for peer in peers:
            meta_copy(peer, peer).wait_send()
            q_copy(peer, peer).wait_send()
        for d in range(n_seq):
            for t in range(n_tp):
                piece_copy(d, t, 0).wait_send()
                stat_copy(d, t, 0).wait_send()

    @pl.when(section == 1)
    def decode():
        pool_copy = pltpu.make_async_copy(pool_hbm, pool, pool_sem)
        for s in range(n_seq):
            for t in range(n_tp):
                pl.semaphore_signal(barrier, inc=1, device_id=at(s, t, 0), device_id_type=MESH)
        for k in range(1, n_tp):
            pl.semaphore_signal(
                barrier, inc=1, device_id=at(seq, lax.rem(tp + k, n_tp), 1), device_id_type=MESH
            )
        for load in loads:
            load.start()
        pool_copy.start()
        for load in loads:
            load.wait()
        pool_copy.wait()
        most = table_ref.shape[2]
        tokens = lax.broadcasted_iota(jnp.int32, (1, most * page), 1)
        for r in range(rows):
            keys = jnp.concatenate([pool[table_ref[r, 0, j]] for j in range(most)], axis=1)
            scores = jnp.dot(q_ref[r], keys, preferred_element_type=jnp.float32) * SOFT_SCALE
            live = tokens < res_ref[0, r]
            scores = jnp.where(live, scores, MASKED)
            row_max = jnp.max(scores, axis=1, keepdims=True)
            e = jnp.where(live, jnp.exp(scores - row_max), 0.0)
            row_total = jnp.sum(e, axis=1, keepdims=True)
            part_out = lax.dot_general(
                e.astype(jnp.bfloat16), keys[:latent],
                (((1,), (1,)), ((), ())), preferred_element_type=jnp.float32,
            )
            for t in range(n_tp):
                mine = slice(t * share, (t + 1) * share)
                for c in range(chunks):
                    res_out[t, r, c * share : (c + 1) * share] = part_out[
                        mine, c * 128 : (c + 1) * 128
                    ]
                res_out[t, r, chunks * share :, :share] = stats_rows(
                    row_max[mine], row_total[mine], 0.0, 0.0
                )
        if n_tp > 1:
            pl.semaphore_wait(barrier, n_tp - 1)
        for k in range(1, n_tp):
            res_copy(lax.rem(tp + k, n_tp), tp).start()
        res_in[tp] = res_out[tp]
        for k in range(1, n_tp):
            peer = lax.rem(tp + k, n_tp)
            res_copy(peer, peer).wait_recv()

        def columns(block):
            wide = jnp.concatenate([block[:, :share], jnp.zeros((8, 128 - share))], axis=1)
            turned = wide.T
            return [turned[:share, i : i + 1] for i in range(4)]

        def joined(block, scale, sums):
            return [
                sums[c] + block[c * share : (c + 1) * share] * scale for c in range(chunks)
            ]

        tail = slice(chunks * share, chunks * share + 8)
        resident = []
        for r in range(rows):
            parts = [columns(res_in[t, r, tail]) for t in range(n_tp)]
            joint = functools.reduce(jnp.maximum, [part[0] for part in parts])
            total = jnp.zeros((share, 1), jnp.float32)
            sums = [jnp.zeros((share, 128), jnp.float32)] * chunks
            for t in range(n_tp):
                scale = jnp.exp(parts[t][0] - joint)
                total += parts[t][1] * scale
                sums = joined(res_in[t, r], scale, sums)
            for c in range(chunks):
                res_sum[r, c * share : (c + 1) * share] = sums[c]
            lines = [res_in[t, r, tail] for t in range(n_tp)]
            joint = functools.reduce(jnp.maximum, [line[0:1] for line in lines])
            total = sum(line[1:2] * jnp.exp(line[0:1] - joint) for line in lines)
            resident.append((joint, total))
        for p in range(n_seq * n_tp):
            stat_copy(0, 0, p).wait_recv()
        count = n_seq * n_tp
        piece_max, piece_total, piece_slot, piece_step = [stat_in[:, i, :] for i in range(4)]
        mixed, kept = [], []
        for r in range(rows):
            row_max, row_total = resident[r]
            member = piece_slot == float(r)
            maxima = jnp.where(member, piece_max, MASKED)
            joint = jnp.maximum(jnp.max(maxima, axis=0, keepdims=True), row_max)
            factor = jnp.exp(row_max - joint)
            factors = jnp.where(member, jnp.exp(maxima - joint), 0.0)
            total = row_total * factor + jnp.sum(piece_total * factors, axis=0, keepdims=True)
            inverse = 1.0 / total
            mixed.append(factors * piece_step * inverse)
            kept.append(factor * inverse)
        used = rows * count + rows
        mixed += kept + [jnp.zeros((-used % 128, 128), jnp.float32)]
        turned = jnp.concatenate(mixed, axis=0).T
        for r in range(rows):
            for p in range(count):
                at_p = r * count + p
                scales[r, p] = jnp.broadcast_to(turned[:share, at_p : at_p + 1], (share, 128))
            at_r = rows * count + r
            factor = turned[:share, at_r : at_r + 1]
            for c in range(chunks):
                block = slice(c * share, (c + 1) * share)
                res_sum[r, block] = res_sum[r, block] * factor
        near = [order[i] * n_tp + t for i in range(2) for t in range(n_tp)]
        far = [order[i] * n_tp + t for i in range(2, n_seq) for t in range(n_tp)]
        for last, arriving in ((False, near), (True, far)):
            for p in arriving:
                piece_copy(0, 0, p).wait_recv()
            for c in range(chunks):
                block = slice(c * share, (c + 1) * share)
                sums = [res_sum[r, block] for r in range(rows)]
                for p in arriving:
                    value = piece_in[p, block].astype(jnp.int32).astype(jnp.float32)
                    sums = [sums[r] + value * scales[r, p] for r in range(rows)]
                for r in range(rows):
                    if last:
                        out_ref[0, r, :, c * 128 : (c + 1) * 128] = sums[r].astype(out_ref.dtype)
                    else:
                        res_sum[r, block] = sums[r]
        for k in range(1, n_tp):
            res_copy(lax.rem(tp + k, n_tp), tp).wait_send()


def local(
    n_seq, n_tp,
    page_pool, queries, block_table, res_len, piece_len, piece_owner, piece_slot, piece_pos, kv_gain
):
    pages, page, width = page_pool.shape
    rows, heads, _ = queries.shape
    latent = kv_gain.shape[0]
    share = heads // n_tp
    packed = latent // 128 * share + 8
    vmem = pl.BlockSpec(memory_space=pltpu.VMEM)
    parts = n_seq * n_tp
    return pl.pallas_call(
        functools.partial(kernel, n_seq, n_tp),
        out_shape=jax.ShapeDtypeStruct((1, rows, share, latent), jnp.bfloat16),
        in_specs=[pl.BlockSpec(memory_space=pltpu.HBM)] * 9,
        out_specs=vmem,
        scratch_shapes=[
            pltpu.VMEM(queries.shape, jnp.bfloat16),
            pltpu.SMEM(block_table.shape, jnp.int32),
            pltpu.SMEM(res_len.shape[::-1], jnp.int32),
            pltpu.SMEM(piece_len.shape, jnp.int32),
            pltpu.SMEM(piece_len.shape, jnp.int32),
            pltpu.SMEM(piece_len.shape, jnp.int32),
            pltpu.SMEM(piece_len.shape, jnp.int32),
            pltpu.VMEM((1, latent), jnp.float32),
            pltpu.SemaphoreType.DMA((8,)),
            pltpu.VMEM((pages, width, page), jnp.bfloat16),
            pltpu.VMEM((width, FRESH_DEV), jnp.bfloat16),
            pltpu.VMEM((n_seq, heads, width), jnp.bfloat16),
            pltpu.VMEM((n_seq, heads, width), jnp.bfloat16),
            pltpu.VMEM((n_seq, 8, 128), jnp.int32),
            pltpu.VMEM((n_seq, 8, 128), jnp.int32),
            pltpu.VMEM((n_seq, n_tp, packed - 8, 128), jnp.int16),
            pltpu.VMEM((parts, packed - 8, 128), jnp.int16),
            pltpu.VMEM((n_seq, n_tp, 8, 128), jnp.float32),
            pltpu.VMEM((parts, 8, 128), jnp.float32),
            pltpu.VMEM((rows, parts, share, 128), jnp.float32),
            pltpu.VMEM((n_tp, rows, packed, 128), jnp.float32),
            pltpu.VMEM((n_tp, rows, packed, 128), jnp.float32),
            pltpu.VMEM((rows, packed, 128), jnp.float32),
            pltpu.SemaphoreType.DMA,
            pltpu.SemaphoreType.DMA((n_seq,)),
            pltpu.SemaphoreType.DMA((n_seq,)),
            pltpu.SemaphoreType.DMA((n_seq,)),
            pltpu.SemaphoreType.DMA((n_seq,)),
            pltpu.SemaphoreType.DMA((parts,)),
            pltpu.SemaphoreType.DMA((parts,)),
            pltpu.SemaphoreType.DMA((parts,)),
            pltpu.SemaphoreType.DMA((parts,)),
            pltpu.SemaphoreType.DMA((n_tp,)),
            pltpu.SemaphoreType.DMA((n_tp,)),
        ],
        compiler_params=pltpu.CompilerParams(
            collective_id=0, has_side_effects=True, vmem_limit_bytes=32 * 1024 * 1024
        ),
    )(
        *[
            pltpu.with_memory_space_constraint(operand, pltpu.HBM)
            for operand in (
                jnp.swapaxes(page_pool, 1, 2), queries, block_table, res_len.T, piece_len,
                piece_owner, piece_slot, piece_pos, kv_gain[None],
            )
        ]
    )


def solution(mesh):
    return jax.shard_map(
        functools.partial(local, mesh.shape["seq"], mesh.shape["tp"]),
        mesh=mesh,
        in_specs=(
            P(("groups", "seq", "tp", "section"), None, None),
            P(("groups", "seq"), None, None),
            P(("groups", "seq"), "tp", None),
            P(("groups", "seq"), "tp"),
            P(("groups", "seq"), "tp", None),
            P(("groups", "seq"), "tp", None),
            P(("groups", "seq"), "tp", None),
            P(("groups", "seq"), "tp", None),
            P(),
        ),
        out_specs=P("section", ("groups", "seq"), "tp", None),
        check_vma=False,
    )
```

```python
import functools

import jax
import jax.numpy as jnp
import numpy as np
from jax import lax
from jax.experimental import pallas as pl
from jax.experimental.pallas import tpu as pltpu
from jax.sharding import PartitionSpec as P

FRESH_DEV = 1024
SOFT_SCALE = 192.0 ** (-0.5)
MASKED = -1e30
NORM_EPSILON = 1e-06
GROUP = 2
STEPS = 32700.0
MESH = pl.DeviceIdType.MESH


def stats_rows(row_max, row_total, slot, step):
    lane = lax.broadcasted_iota(jnp.int32, (row_max.shape[0], 128), 1)
    block = jnp.where(
        lane == 0, row_max, jnp.where(lane == 1, row_total, jnp.where(lane == 2, slot, step))
    )
    return block.T[:8]


def cos_sin(angles):
    turns = jnp.floor(angles * (2.0 / np.pi) + 0.5)
    rest = angles - turns * 1.5703125
    rest = rest - turns * 4.837512969970703125e-4
    rest = rest - turns * 7.54978995489188216e-8
    square = rest * rest
    sine = rest + rest * square * (
        -1.6666654611e-1 + square * (8.3321608736e-3 + square * -1.9515295891e-4)
    )
    cosine = (
        1.0
        - 0.5 * square
        + square * square
        * (4.166664568298827e-2 + square * (-1.388731625493765e-3 + square * 2.443315711809948e-5))
    )
    quarter = turns.astype(jnp.int32) & 3
    odd = (quarter & 1) == 1
    cos_value = jnp.where(odd, sine, cosine)
    sin_value = jnp.where(odd, cosine, sine)
    cos_value = jnp.where((quarter == 1) | (quarter == 2), -cos_value, cos_value)
    sin_value = jnp.where(quarter >= 2, -sin_value, sin_value)
    return cos_value, sin_value


def kernel(
    n_seq, n_tp, pool_hbm, q_hbm, table_hbm, res_hbm, len_hbm, owner_hbm, slot_hbm, pos_hbm,
    gain_hbm, out_ref,
    q_ref, table_ref, res_ref, len_ref, owner_ref, slot_ref, pos_ref, gain_ref, load_sem,
    pool, fresh, q_in, q_out, meta_in, meta_out, piece_out, piece_in, stat_out, stat_in, scales, res_out, res_in, res_sum,
    pool_sem, meta_send, meta_recv, q_send, q_recv, piece_send, piece_recv, stat_send, stat_recv,
    res_send, res_recv,
):
    pages, width, page = pool.shape
    rows, heads, _ = q_ref.shape
    latent = gain_ref.shape[1]
    half = (width - latent) // 2
    share = heads // n_tp
    fresh_pages = FRESH_DEV // page
    chunks = latent // 128
    seq = lax.axis_index("seq")
    tp = lax.axis_index("tp")
    section = lax.axis_index("section")
    barrier = pltpu.get_barrier_semaphore()
    order = [lax.rem((seq // 2) * 2 + i, n_seq) for i in range(n_seq)]
    peers = [(seq // 2) * 2 + 1 - lax.rem(seq, 2)] + order[2:]

    loads = [
        pltpu.make_async_copy(source, target, load_sem.at[i])
        for i, (source, target) in enumerate(
            [
                (len_hbm, len_ref), (owner_hbm, owner_ref), (slot_hbm, slot_ref),
                (pos_hbm, pos_ref), (table_hbm, table_ref), (res_hbm, res_ref),
                (q_hbm, q_ref), (gain_hbm, gain_ref),
            ]
        )
    ]
    def at(s, t, c):
        return {"seq": s, "tp": t, "section": c}

    def meta_copy(peer, own):
        return pltpu.make_async_remote_copy(
            meta_out.at[peer], meta_in.at[own], meta_send.at[peer], meta_recv.at[own],
            device_id=at(peer, tp, 0), device_id_type=MESH,
        )

    def q_copy(peer, own):
        return pltpu.make_async_remote_copy(
            q_out.at[peer], q_in.at[own], q_send.at[peer], q_recv.at[own],
            device_id=at(peer, tp, 0), device_id_type=MESH,
        )

    def piece_copy(i, t, own):
        return pltpu.make_async_remote_copy(
            piece_out.at[i, t], piece_in.at[own], piece_send.at[i * n_tp + t], piece_recv.at[own],
            device_id=at(order[i], t, 1), device_id_type=MESH,
        )

    def stat_copy(i, t, own):
        return pltpu.make_async_remote_copy(
            stat_out.at[i, t], stat_in.at[own], stat_send.at[i * n_tp + t], stat_recv.at[own],
            device_id=at(order[i], t, 1), device_id_type=MESH,
        )

    def res_copy(t, own):
        return pltpu.make_async_remote_copy(
            res_out.at[t], res_in.at[own], res_send.at[t], res_recv.at[own],
            device_id=at(seq, t, 1), device_id_type=MESH,
        )

    @pl.when(section == 0)
    def prefill():
        raw_copy = pltpu.make_async_copy(
            pool_hbm.at[pl.ds(0, fresh_pages)], pool.at[pl.ds(0, fresh_pages)], pool_sem
        )
        for peer in peers:
            pl.semaphore_signal(barrier, inc=1, device_id=at(peer, tp, 0), device_id_type=MESH)
        for load in loads:
            load.start()
        raw_copy.start()
        for load in loads:
            load.wait()

        lengths = [len_ref[0, 0, k] for k in range(n_seq)]
        begins = [jnp.int32(0)]
        for k in range(n_seq - 1):
            begins.append(begins[-1] + lengths[k])

        def of_owner(d, values):
            total = jnp.int32(0)
            for k in range(n_seq):
                total = total + jnp.where(owner_ref[0, 0, k] == d, values[k], 0)
            return total

        slots = [slot_ref[0, 0, k] for k in range(n_seq)]
        owner_begin = [of_owner(d, begins) for d in order]
        owner_len = [of_owner(d, lengths) for d in order]
        owner_slot = [of_owner(d, slots) for d in order]
        for i, d in enumerate(order):
            meta_out[d] = jnp.full(meta_out.shape[1:], owner_slot[i], jnp.int32)

        pl.semaphore_wait(barrier, n_seq - 1 + n_seq * n_tp)
        for peer in peers[1:] + peers[:1]:
            meta_copy(peer, seq).start()

        for peer in peers[1:] + peers[:1]:
            meta_copy(peer, peer).wait_recv()
            wanted = meta_in[peer][0:1, 0:1]
            picked = q_ref[0].astype(jnp.float32)
            for r in range(1, rows):
                picked = jnp.where(wanted == r, q_ref[r].astype(jnp.float32), picked)
            q_out[peer] = picked.astype(jnp.bfloat16)
            q_copy(peer, seq).start()
        own_slot = meta_out[seq][0:1, 0:1]
        picked = q_ref[0].astype(jnp.float32)
        for r in range(1, rows):
            picked = jnp.where(own_slot == r, q_ref[r].astype(jnp.float32), picked)
        q_in[seq] = picked.astype(jnp.bfloat16)

        out_ref[...] = jnp.zeros_like(out_ref)
        raw_copy.wait()
        gain = jnp.broadcast_to(gain_ref[...], (page, latent)).T
        index = lax.broadcasted_iota(jnp.int32, (half, page), 0)
        freq = jnp.ones((half, page), jnp.float32)
        for i in range(1, half):
            freq = jnp.where(index == i, float(10000.0 ** (-i / half)), freq)
        for j in range(fresh_pages):
            x = pool[j, :latent].astype(jnp.float32)
            mean = jnp.mean(x * x, axis=0, keepdims=True)
            columns = slice(j * page, (j + 1) * page)
            normed = x * lax.rsqrt(mean + NORM_EPSILON) * gain
            fresh[:latent, columns] = normed.astype(jnp.bfloat16)
            y = pool[j, latent:].astype(jnp.float32)
            a, b = y[:half], y[half:]
            token = lax.broadcasted_iota(jnp.int32, (1, page), 1) + j * page
            shift = jnp.zeros((1, page), jnp.int32)
            for k in range(n_seq):
                live = (token >= begins[k]) & (token < begins[k] + lengths[k])
                shift = jnp.where(live, pos_ref[0, 0, k] - begins[k], shift)
            cosine, sine = cos_sin((token + shift).astype(jnp.float32) * freq)
            turned = jnp.concatenate([a * cosine - b * sine, b * cosine + a * sine], axis=0)
            fresh[latent:, columns] = turned.astype(jnp.bfloat16)

        out_ref[...] = jnp.zeros_like(out_ref)
        tokens = lax.broadcasted_iota(jnp.int32, (1, FRESH_DEV), 1)
        for first in range(0, n_seq, GROUP):
            for d in peers[max(first - 1, 0) : first + GROUP - 1]:
                q_copy(d, d).wait_recv()
            members = range(first, first + GROUP)
            wide = jnp.concatenate([q_in[order[i]] for i in members], axis=0)
            scores = jnp.dot(wide, fresh[...], preferred_element_type=jnp.float32) * SOFT_SCALE
            stats = []
            weights = []
            for i in members:
                live = (tokens >= owner_begin[i]) & (tokens < owner_begin[i] + owner_len[i])
                here = (i - first) * heads
                part = jnp.where(live, scores[here : here + heads], MASKED)
                row_max = jnp.max(part, axis=1, keepdims=True)
                e = jnp.where(live, jnp.exp(part - row_max), 0.0)
                row_total = jnp.sum(e, axis=1, keepdims=True)
                weights.append(e.astype(jnp.bfloat16))
                stats.append((row_max, row_total, owner_slot[i].astype(jnp.float32)))
            group_out = lax.dot_general(
                jnp.concatenate(weights, axis=0), fresh[:latent],
                (((1,), (1,)), ((), ())), preferred_element_type=jnp.float32,
            )
            step = jnp.maximum(jnp.max(jnp.abs(group_out), axis=1, keepdims=True), 1e-30) / STEPS
            turned = stats_rows(
                jnp.concatenate([stats[i - first][0] for i in members], axis=0),
                jnp.concatenate([stats[i - first][1] for i in members], axis=0),
                jnp.concatenate(
                    [jnp.full((heads, 1), stats[i - first][2], jnp.float32) for i in members],
                    axis=0,
                ),
                step,
            )
            for i in members:
                for t in range(n_tp):
                    here = (i - first) * heads + t * share
                    stat_out[i, t, :, :share] = turned[:, here : here + share]
                    stat_copy(i, t, seq * n_tp + tp).start()
            counted = jnp.floor(group_out * (1.0 / step) + 0.5)
            for i in members:
                for t in range(n_tp):
                    here = (i - first) * heads + t * share
                    stacked = jnp.concatenate(
                        [
                            counted[here : here + share, c * 128 : (c + 1) * 128]
                            for c in range(chunks)
                        ],
                        axis=0,
                    )
                    piece_out[i, t] = stacked.astype(jnp.int32).astype(jnp.int16)
                    piece_copy(i, t, seq * n_tp + tp).start()

        for peer in peers:
            meta_copy(peer, peer).wait_send()
            q_copy(peer, peer).wait_send()
        for d in range(n_seq):
            for t in range(n_tp):
                piece_copy(d, t, 0).wait_send()
                stat_copy(d, t, 0).wait_send()

    @pl.when(section == 1)
    def decode():
        pool_copy = pltpu.make_async_copy(pool_hbm, pool, pool_sem)
        for s in range(n_seq):
            for t in range(n_tp):
                pl.semaphore_signal(barrier, inc=1, device_id=at(s, t, 0), device_id_type=MESH)
        for k in range(1, n_tp):
            pl.semaphore_signal(
                barrier, inc=1, device_id=at(seq, lax.rem(tp + k, n_tp), 1), device_id_type=MESH
            )
        for load in loads:
            load.start()
        pool_copy.start()
        for load in loads:
            load.wait()
        pool_copy.wait()
        most = table_ref.shape[2]
        tokens = lax.broadcasted_iota(jnp.int32, (1, most * page), 1)
        for r in range(rows):
            keys = jnp.concatenate([pool[table_ref[r, 0, j]] for j in range(most)], axis=1)
            scores = jnp.dot(q_ref[r], keys, preferred_element_type=jnp.float32) * SOFT_SCALE
            live = tokens < res_ref[0, r]
            scores = jnp.where(live, scores, MASKED)
            row_max = jnp.max(scores, axis=1, keepdims=True)
            e = jnp.where(live, jnp.exp(scores - row_max), 0.0)
            row_total = jnp.sum(e, axis=1, keepdims=True)
            part_out = lax.dot_general(
                e.astype(jnp.bfloat16), keys[:latent],
                (((1,), (1,)), ((), ())), preferred_element_type=jnp.float32,
            )
            for t in range(n_tp):
                mine = slice(t * share, (t + 1) * share)
                for c in range(chunks):
                    res_out[t, r, c * share : (c + 1) * share] = part_out[
                        mine, c * 128 : (c + 1) * 128
                    ]
                res_out[t, r, chunks * share :, :share] = stats_rows(
                    row_max[mine], row_total[mine], 0.0, 0.0
                )
        if n_tp > 1:
            pl.semaphore_wait(barrier, n_tp - 1)
        for k in range(1, n_tp):
            res_copy(lax.rem(tp + k, n_tp), tp).start()
        res_in[tp] = res_out[tp]
        for k in range(1, n_tp):
            peer = lax.rem(tp + k, n_tp)
            res_copy(peer, peer).wait_recv()

        def columns(block):
            wide = jnp.concatenate([block[:, :share], jnp.zeros((8, 128 - share))], axis=1)
            turned = wide.T
            return [turned[:share, i : i + 1] for i in range(4)]

        def joined(block, scale, sums):
            return [
                sums[c] + block[c * share : (c + 1) * share] * scale for c in range(chunks)
            ]

        tail = slice(chunks * share, chunks * share + 8)
        resident = []
        for r in range(rows):
            parts = [columns(res_in[t, r, tail]) for t in range(n_tp)]
            joint = functools.reduce(jnp.maximum, [part[0] for part in parts])
            total = jnp.zeros((share, 1), jnp.float32)
            sums = [jnp.zeros((share, 128), jnp.float32)] * chunks
            for t in range(n_tp):
                scale = jnp.exp(parts[t][0] - joint)
                total += parts[t][1] * scale
                sums = joined(res_in[t, r], scale, sums)
            for c in range(chunks):
                res_sum[r, c * share : (c + 1) * share] = sums[c]
            lines = [res_in[t, r, tail] for t in range(n_tp)]
            joint = functools.reduce(jnp.maximum, [line[0:1] for line in lines])
            total = sum(line[1:2] * jnp.exp(line[0:1] - joint) for line in lines)
            resident.append((joint, total))
        for p in range(n_seq * n_tp):
            stat_copy(0, 0, p).wait_recv()
        count = n_seq * n_tp
        piece_max, piece_total, piece_slot, piece_step = [stat_in[:, i, :] for i in range(4)]
        mixed, kept = [], []
        for r in range(rows):
            row_max, row_total = resident[r]
            member = piece_slot == float(r)
            maxima = jnp.where(member, piece_max, MASKED)
            joint = jnp.maximum(jnp.max(maxima, axis=0, keepdims=True), row_max)
            factor = jnp.exp(row_max - joint)
            factors = jnp.where(member, jnp.exp(maxima - joint), 0.0)
            total = row_total * factor + jnp.sum(piece_total * factors, axis=0, keepdims=True)
            inverse = 1.0 / total
            mixed.append(factors * piece_step * inverse)
            kept.append(factor * inverse)
        used = rows * count + rows
        mixed += kept + [jnp.zeros((-used % 128, 128), jnp.float32)]
        turned = jnp.concatenate(mixed, axis=0).T
        for r in range(rows):
            for p in range(count):
                at_p = r * count + p
                scales[r, p] = jnp.broadcast_to(turned[:share, at_p : at_p + 1], (share, 128))
            at_r = rows * count + r
            factor = turned[:share, at_r : at_r + 1]
            for c in range(chunks):
                block = slice(c * share, (c + 1) * share)
                res_sum[r, block] = res_sum[r, block] * factor
        for p in range(n_seq * n_tp):
            piece_copy(0, 0, p).wait_recv()
        for c in range(chunks):
            block = slice(c * share, (c + 1) * share)
            sums = [res_sum[r, block] for r in range(rows)]
            for p in range(n_seq * n_tp):
                value = piece_in[p][block].astype(jnp.int32).astype(jnp.float32)
                sums = [sums[r] + value * scales[r, p] for r in range(rows)]
            for r in range(rows):
                out_ref[0, r, :, c * 128 : (c + 1) * 128] = sums[r].astype(out_ref.dtype)
        for k in range(1, n_tp):
            res_copy(lax.rem(tp + k, n_tp), tp).wait_send()


def local(
    n_seq, n_tp,
    page_pool, queries, block_table, res_len, piece_len, piece_owner, piece_slot, piece_pos, kv_gain
):
    pages, page, width = page_pool.shape
    rows, heads, _ = queries.shape
    latent = kv_gain.shape[0]
    share = heads // n_tp
    packed = latent // 128 * share + 8
    vmem = pl.BlockSpec(memory_space=pltpu.VMEM)
    parts = n_seq * n_tp
    return pl.pallas_call(
        functools.partial(kernel, n_seq, n_tp),
        out_shape=jax.ShapeDtypeStruct((1, rows, share, latent), jnp.bfloat16),
        in_specs=[pl.BlockSpec(memory_space=pltpu.HBM)] * 9,
        out_specs=vmem,
        scratch_shapes=[
            pltpu.VMEM(queries.shape, jnp.bfloat16),
            pltpu.SMEM(block_table.shape, jnp.int32),
            pltpu.SMEM(res_len.shape[::-1], jnp.int32),
            pltpu.SMEM(piece_len.shape, jnp.int32),
            pltpu.SMEM(piece_len.shape, jnp.int32),
            pltpu.SMEM(piece_len.shape, jnp.int32),
            pltpu.SMEM(piece_len.shape, jnp.int32),
            pltpu.VMEM((1, latent), jnp.float32),
            pltpu.SemaphoreType.DMA((8,)),
            pltpu.VMEM((pages, width, page), jnp.bfloat16),
            pltpu.VMEM((width, FRESH_DEV), jnp.bfloat16),
            pltpu.VMEM((n_seq, heads, width), jnp.bfloat16),
            pltpu.VMEM((n_seq, heads, width), jnp.bfloat16),
            pltpu.VMEM((n_seq, 8, 128), jnp.int32),
            pltpu.VMEM((n_seq, 8, 128), jnp.int32),
            pltpu.VMEM((n_seq, n_tp, packed - 8, 128), jnp.int16),
            pltpu.VMEM((parts, packed - 8, 128), jnp.int16),
            pltpu.VMEM((n_seq, n_tp, 8, 128), jnp.float32),
            pltpu.VMEM((parts, 8, 128), jnp.float32),
            pltpu.VMEM((rows, parts, share, 128), jnp.float32),
            pltpu.VMEM((n_tp, rows, packed, 128), jnp.float32),
            pltpu.VMEM((n_tp, rows, packed, 128), jnp.float32),
            pltpu.VMEM((rows, packed, 128), jnp.float32),
            pltpu.SemaphoreType.DMA,
            pltpu.SemaphoreType.DMA((n_seq,)),
            pltpu.SemaphoreType.DMA((n_seq,)),
            pltpu.SemaphoreType.DMA((n_seq,)),
            pltpu.SemaphoreType.DMA((n_seq,)),
            pltpu.SemaphoreType.DMA((parts,)),
            pltpu.SemaphoreType.DMA((parts,)),
            pltpu.SemaphoreType.DMA((parts,)),
            pltpu.SemaphoreType.DMA((parts,)),
            pltpu.SemaphoreType.DMA((n_tp,)),
            pltpu.SemaphoreType.DMA((n_tp,)),
        ],
        compiler_params=pltpu.CompilerParams(
            collective_id=0, has_side_effects=True, vmem_limit_bytes=32 * 1024 * 1024
        ),
    )(
        *[
            pltpu.with_memory_space_constraint(operand, pltpu.HBM)
            for operand in (
                jnp.swapaxes(page_pool, 1, 2), queries, block_table, res_len.T, piece_len,
                piece_owner, piece_slot, piece_pos, kv_gain[None],
            )
        ]
    )


def solution(mesh):
    return jax.shard_map(
        functools.partial(local, mesh.shape["seq"], mesh.shape["tp"]),
        mesh=mesh,
        in_specs=(
            P(("groups", "seq", "tp", "section"), None, None),
            P(("groups", "seq"), None, None),
            P(("groups", "seq"), "tp", None),
            P(("groups", "seq"), "tp"),
            P(("groups", "seq"), "tp", None),
            P(("groups", "seq"), "tp", None),
            P(("groups", "seq"), "tp", None),
            P(("groups", "seq"), "tp", None),
            P(),
        ),
        out_specs=P("section", ("groups", "seq"), "tp", None),
        check_vma=False,
    )
```
